128 devices in a mesh: grp: 4 (over y), dev: 32 (over z, x, core).
Axes of the slice: x: 4, y: 4, z: 4, core: 2. Of those that a mesh axis runs over, the one named last changes fastest.
Arguments:
- states: bfloat16 [16, 256, 4096], P('grp', 'dev'), may hold values from -6 to 6
- query_in: bfloat16 [16, 256, 4096], P('grp', 'dev'), may hold values from -6 to 6
- key_in: bfloat16 [16, 256, 1024], P('grp', 'dev'), may hold values from -6 to 6
- value_in: bfloat16 [16, 256, 1024], P('grp', 'dev'), may hold values from -6 to 6
- cached_delta: bfloat16 [16, 256, 4096], P('grp', 'dev'), may hold values from -4 to 4
- recompute: int32 [16], P('grp'), may hold values from 0 to 1, as said below
- expert_ids: int32 [4096, 8], P(('grp', 'dev')), may hold values from 0 to 31, as said below
- expert_weights: float32 [4096, 8], P(('grp', 'dev')), may hold values from 0.1 to 1
- norm_gain: float32 [4096], replicated, may hold values from 0.1 to 1.9
- out_proj: bfloat16 [4096, 4096], P('dev'), may hold values from -0.5 to 0.5
- gate_proj: bfloat16 [32, 4096, 3072], P('dev', None, 'grp'), may hold values from -0.09375 to 0.09375
- up_proj: bfloat16 [32, 4096, 3072], P('dev', None, 'grp'), may hold values from -0.09375 to 0.09375
- down_proj: bfloat16 [32, 3072, 4096], P('dev', 'grp'), may hold values from -0.109375 to 0.109375
Outputs:
- layer_out: bfloat16 [16, 256, 4096], P('grp', 'dev')
The draws below stay inside these ranges and needn't reach their ends.
Inputs may be any that keep to these rules, and one draw needn't show every extreme that they name: `recompute`: 1 marks a recomputed request, 0 one whose cached change is reused; the 4 consecutive requests of one index of grp hold 2 to 3 recomputed ones, and some index holds exactly 3. `expert_ids`: each row names 8 different experts; in each aligned block of 32 rows (the rows of one device) no expert is named by more than 10 rows, and some expert by exactly 10.
All inputs are finite; a program needn't handle non-finite values.
Results may differ from the reference program's by a relative error of at most 0.024.
Values may be sent and summed in bfloat16 or wider, within the bound.
A program may use at most 128 MiB of HBM per device.

```python
import math
import jax
import jax.numpy as jnp
from jax import lax

D = 4096
HEADS = 32
KV_HEADS = 8
DH = 128
FF = 3072
TOPK = 8
SEQ_DEV = 8
REQ_GRP = 4
ACT_GRP = 3
LEN = 256
REQS = 16
TOKENS = 4096
ROWS_DEV = 32
EXPERTS = 32
CAP = 10
N_GRP = 4
N_DEV = 32


def live_requests(key):
    groups = REQS // REQ_GRP
    counts = jax.random.randint(jax.random.fold_in(key, 11), (groups,), max(1, ACT_GRP - 1), ACT_GRP + 1)
    fullest = jax.random.randint(jax.random.fold_in(key, 12), (), 0, groups)
    counts = jnp.where(jnp.arange(groups) == fullest, ACT_GRP, counts)
    scores = jax.random.randint(jax.random.fold_in(key, 13), (groups, REQ_GRP), 0, 1024) * REQ_GRP + jnp.arange(REQ_GRP)[None, :]
    ranking = jnp.argsort(jnp.argsort(scores, axis=1), axis=1)
    return (ranking < counts[:, None]).astype(jnp.int32)


def route_table(key):
    groups = REQS // REQ_GRP
    live = live_requests(key)
    live_rows = jnp.repeat(live, SEQ_DEV, axis=1)
    span = jnp.maximum(SEQ_DEV * jnp.sum(live, axis=1), CAP).astype(jnp.int32)
    hot_count = 2 * span // CAP
    cold_count = EXPERTS - hot_count
    span_all = span[:, None, None, None]
    hot_all = hot_count[:, None, None, None]
    cold_all = cold_count[:, None, None, None]
    route_key = jax.random.fold_in(key, 21)
    noise = jax.random.randint(jax.random.fold_in(route_key, 1), (groups, EXPERTS, ROWS_DEV), 0, 1024)
    score = ((1 - live_rows[:, None, :]) * 1024 + noise) * ROWS_DEV + jnp.arange(ROWS_DEV, dtype=jnp.int32)[None, None, :]
    rank = jnp.argsort(jnp.argsort(score, axis=-1), axis=-1).astype(jnp.int32)[..., None]
    column = jnp.arange(TOPK, dtype=jnp.int32)[None, None, None, :]
    ticket = column * ROWS_DEV + rank
    cold_index = ticket * cold_all // (TOPK * ROWS_DEV)
    rotation = jax.random.randint(jax.random.fold_in(route_key, 2), (groups, EXPERTS, 1, 1), 0, 1 << 20) % cold_all
    cold_slot = hot_all + (cold_index + rotation) % cold_all
    hot_index = (column * span_all + rank) // CAP
    is_hot = (column < 2) & (rank < span_all) & (hot_index < hot_all)
    slot = jnp.where(is_hot, hot_index, cold_slot).astype(jnp.int32)
    order_scores = jax.random.randint(jax.random.fold_in(route_key, 3), (groups, EXPERTS), 0, 1 << 20) * EXPERTS + jnp.arange(EXPERTS, dtype=jnp.int32)[None, :]
    orders = jnp.argsort(order_scores, axis=1).astype(jnp.int32)
    named = jnp.take_along_axis(orders, slot.reshape(groups, -1), axis=1).reshape(groups, EXPERTS, ROWS_DEV, TOPK)
    shuffle_scores = jax.random.randint(jax.random.fold_in(route_key, 4), (groups, EXPERTS, ROWS_DEV, TOPK), 0, 1024) * TOPK + column
    shuffle = jnp.argsort(shuffle_scores, axis=-1)
    named = jnp.take_along_axis(named, shuffle, axis=-1)
    heavy = jnp.take_along_axis(is_hot, shuffle, axis=-1)
    return (named.reshape(groups * EXPERTS * ROWS_DEV, TOPK).astype(jnp.int32), heavy.reshape(groups * EXPERTS * ROWS_DEV, TOPK))


def draw_query_in(key, part):
    sample = jnp.clip(1.5 * jax.random.normal(jax.random.fold_in(key, 1), (REQS, LEN, HEADS, DH), jnp.float32), -6.0, 6.0)
    return sample.reshape(REQS, LEN, HEADS * DH).astype(jnp.bfloat16)


def draw_key_in(key, part):
    sample = jnp.clip(jax.random.normal(jax.random.fold_in(key, 2), (REQS, LEN, KV_HEADS, DH), jnp.float32), -6.0, 6.0)
    return sample.reshape(REQS, LEN, KV_HEADS * DH).astype(jnp.bfloat16)


def draw_recompute(key, part):
    return live_requests(key).reshape(REQS)


def draw_expert_ids(key, part):
    named, heavy = route_table(key)
    return named


def draw_expert_weights(key, part):
    named, heavy = route_table(key)
    key = jax.random.fold_in(key, 31)
    spread = jax.random.uniform(jax.random.fold_in(key, 1), named.shape, jnp.float32, 0.1, 1.0)
    strong = jax.random.uniform(jax.random.fold_in(key, 2), named.shape, jnp.float32, 0.8, 1.0)
    return jnp.where(heavy, strong, spread).astype(jnp.float32)


def block_scale(stream_key, extent, split, least, largest):
    factor_of, own = 1.0, jax.random.fold_in(stream_key, 6)
    for axis_at, shards_of in split:
        steps = jnp.exp(jax.random.uniform(jax.random.fold_in(own, axis_at), (shards_of,), jnp.float32, least / len(split), largest / len(split)))
        factor_of = factor_of * jnp.repeat(steps, extent[axis_at] // shards_of).reshape([-1 if axis == axis_at else 1 for axis in range(len(extent))])
    return factor_of


def scatter_about(stream_key, dims, deviation, bound, pieces=(), held_as=jnp.bfloat16):
    values = jax.random.normal(stream_key, dims, jnp.float32) * deviation
    if len(pieces) > 0:
        values = block_scale(stream_key, dims, pieces, -0.22, 0.18) * values
    return jnp.clip(values, min=-bound, max=bound).astype(held_as)


def setup_inputs(seed: int = 0) -> dict:
    key_list = jax.random.split(jax.random.key(seed), 14)
    states = scatter_about(key_list[0], (REQS, LEN, D), 1.0, 6.0, ((0, 4), (1, 32)))
    query_in = draw_query_in(jax.random.fold_in(key_list[13], 71), 0)
    key_in = draw_key_in(jax.random.fold_in(key_list[13], 71), 0)
    value_in = scatter_about(key_list[3], (REQS, LEN, KV_HEADS * DH), 1.0, 6.0, ((0, 4), (1, 32)))
    cached_delta = scatter_about(key_list[4], (REQS, LEN, D), 0.5, 4.0, ((0, 4), (1, 32)))
    recompute = draw_recompute(jax.random.fold_in(key_list[13], 71), 0)
    expert_ids = draw_expert_ids(jax.random.fold_in(key_list[13], 71), 0)
    expert_weights = draw_expert_weights(jax.random.fold_in(key_list[13], 71), 0)
    norm_gain = jnp.clip(1.0 + 0.18 * jax.random.normal(key_list[8], (D,), jnp.float32), 0.1, 1.9)
    out_proj = scatter_about(key_list[9], (HEADS * DH, D), DH ** -0.5, 0.5, ((0, 32),))
    gate_proj = scatter_about(key_list[10], (EXPERTS, D, FF), D ** -0.5, 0.09375, ((0, 32), (2, 4)))
    up_proj = scatter_about(key_list[11], (EXPERTS, D, FF), D ** -0.5, 0.09375, ((0, 32), (2, 4)))
    down_proj = scatter_about(key_list[12], (EXPERTS, FF, D), FF ** -0.5, 0.109375, ((0, 32), (1, 4)))
    return {"states": states, "query_in": query_in, "key_in": key_in, "value_in": value_in, "cached_delta": cached_delta, "recompute": recompute, "expert_ids": expert_ids, "expert_weights": expert_weights, "norm_gain": norm_gain, "out_proj": out_proj, "gate_proj": gate_proj, "up_proj": up_proj, "down_proj": down_proj}


def reference(states, query_in, key_in, value_in, cached_delta, recompute, expert_ids, expert_weights, norm_gain, out_proj, gate_proj, up_proj, down_proj):
    group_size = HEADS // KV_HEADS
    queries = query_in.astype(jnp.float32).reshape(REQS, LEN, HEADS, DH)
    keys_all = jnp.repeat(key_in.astype(jnp.float32).reshape(REQS, LEN, KV_HEADS, DH), group_size, axis=2)
    values_all = jnp.repeat(value_in.astype(jnp.float32).reshape(REQS, LEN, KV_HEADS, DH), group_size, axis=2)
    scores = jnp.einsum('rqhd,rkhd->rhqk', queries, keys_all) * (1.0 / math.sqrt(DH))
    highest = lax.optimization_barrier(jnp.max(scores, axis=-1, keepdims=True))
    raised = jnp.exp(scores - highest)
    attn_weights = (raised / lax.optimization_barrier(jnp.sum(raised, axis=-1, keepdims=True))).astype(jnp.bfloat16)
    mixed_heads = jnp.einsum('rhqk,rkhd->rqhd', attn_weights.astype(jnp.float32), values_all).astype(jnp.bfloat16)
    attn_out = jnp.dot(mixed_heads.reshape(TOKENS, HEADS * DH), out_proj, preferred_element_type=jnp.float32)
    residual = states.astype(jnp.float32).reshape(TOKENS, D) + attn_out
    mean_square = lax.optimization_barrier(jnp.mean(residual * residual, axis=-1, keepdims=True))
    normed = (residual * lax.rsqrt(mean_square + 1e-06) * norm_gain).astype(jnp.bfloat16)
    routed_ids = expert_ids.reshape(N_GRP, N_DEV, REQ_GRP, SEQ_DEV, TOPK).transpose(0, 2, 1, 3, 4).reshape(TOKENS, TOPK)
    routed_weights = expert_weights.reshape(N_GRP, N_DEV, REQ_GRP, SEQ_DEV, TOPK).transpose(0, 2, 1, 3, 4).reshape(TOKENS, TOPK)
    live_tokens = jnp.repeat(recompute, LEN)
    slice_width = FF // N_GRP
    slot_limit = N_GRP * N_DEV * CAP

    def one_expert(running, stacked):
        expert_index, gate_w, up_w, down_w = stacked
        chosen_pair = (routed_ids == expert_index) & (live_tokens[:, None] == 1)
        token_hit = jnp.any(chosen_pair, axis=1)
        token_weight = lax.optimization_barrier(jnp.sum(jnp.where(chosen_pair, routed_weights, 0.0), axis=1))
        where_rows = jnp.nonzero(token_hit, size=slot_limit, fill_value=0)[0].astype(jnp.int32)
        filled = jnp.arange(slot_limit) < jnp.sum(token_hit.astype(jnp.int32))
        routed_rows = jnp.take(normed, where_rows, axis=0)
        summed = jnp.zeros((slot_limit, D), jnp.float32)
        for grp_index in range(N_GRP):
            first_col = grp_index * slice_width
            gate_val = jnp.dot(routed_rows, gate_w[:, first_col:first_col + slice_width], preferred_element_type=jnp.float32)
            up_val = jnp.dot(routed_rows, up_w[:, first_col:first_col + slice_width], preferred_element_type=jnp.float32)
            hidden_val = (jax.nn.silu(gate_val) * up_val).astype(jnp.bfloat16)
            partial_out = jnp.dot(hidden_val, down_w[first_col:first_col + slice_width, :], preferred_element_type=jnp.float32)
            summed = summed + lax.optimization_barrier(partial_out.astype(jnp.bfloat16)).astype(jnp.float32)
        expert_out = lax.optimization_barrier(summed.astype(jnp.bfloat16)).astype(jnp.float32)
        scale_rows = jnp.where(filled, jnp.take(token_weight, where_rows, axis=0), 0.0)
        added = expert_out * scale_rows[:, None]
        return (running.at[where_rows].add(added), None)
    moe_zero = jnp.zeros((TOKENS, D), jnp.float32)
    moe, unused = lax.scan(one_expert, moe_zero, (jnp.arange(EXPERTS, dtype=jnp.int32), gate_proj, up_proj, down_proj))
    reused = states.astype(jnp.float32).reshape(TOKENS, D) + cached_delta.astype(jnp.float32).reshape(TOKENS, D)
    layer_out = jnp.where((live_tokens == 1)[:, None], residual + moe, reused)
    return layer_out.astype(jnp.bfloat16).reshape(REQS, LEN, D)
```

```python
import math

import jax
import jax.numpy as jnp
from jax import lax
from jax.experimental import pallas as pl
from jax.experimental.pallas import tpu as pltpu
from jax.sharding import PartitionSpec as P

HEADS = 32
KV_HEADS = 8
DH = 128
SLOTS = 3
BF = jnp.bfloat16
F32 = jnp.float32
MESH = pl.DeviceIdType.MESH
ORDER = (("x", "z", "y"), ("z", "y", "x"), ("y", "x", "z"))


def mod4(v):
    return lax.rem(v + 4, 4)


class Place:
    def __init__(self):
        self.y = lax.axis_index("grp")
        dev = lax.axis_index("dev")
        self.core = lax.rem(dev, 2)
        self.x = lax.rem(lax.div(dev, 2), 4)
        self.z = lax.div(dev, 8)

    def at(self, axis):
        return {"x": self.x, "y": self.y, "z": self.z}[axis]

    def to(self, axis, step):
        y, x, z = self.y, self.x, self.z
        if axis == "y":
            y = mod4(y + step)
        elif axis == "x":
            x = mod4(x + step)
        else:
            z = mod4(z + step)
        return (y, (z * 4 + x) * 2 + self.core)

    def sibling(self):
        return (self.y, (self.z * 4 + self.x) * 2 + 1 - self.core)

    def greet(self, axes):
        barrier = pltpu.get_barrier_semaphore()
        others = [self.to(axis, step) for axis in axes for step in (1, -1)]
        others.append(self.sibling())
        for other in others:
            pl.semaphore_signal(barrier, inc=1, device_id=other, device_id_type=MESH)
        pl.semaphore_wait(barrier, len(others))


class Copies:
    def __init__(self, send_sem, recv_sem):
        self.send_sem, self.recv_sem = send_sem, recv_sem
        self.made = []

    def start(self, src, dst, device):
        k = len(self.made)
        copy = pltpu.make_async_remote_copy(
            src_ref=src,
            dst_ref=dst,
            send_sem=self.send_sem.at[k],
            recv_sem=self.recv_sem.at[k],
            device_id=device,
            device_id_type=MESH,
        )
        copy.start()
        self.made.append(copy)
        return copy

    def finish(self):
        for copy in self.made:
            copy.wait_send()


def gather_kernel(
    norm_ref, gw_ref, gate_hbm, up_hbm, down_hbm,
    hid_out, dsib_out,
    tok, xbuf, wg, wu, hid, send_sem, recv_sem, load_sem, hsend_sem, hrecv_sem, hloc_sem,
):
    here = Place()
    c = here.core
    sib = here.sibling()
    load_g = pltpu.make_async_copy(gate_hbm, wg, load_sem.at[0])
    load_u = pltpu.make_async_copy(up_hbm, wu, load_sem.at[1])
    load_g.start()
    load_u.start()
    here.greet(("x", "y", "z"))
    copies = Copies(send_sem, recv_sem)
    m1 = [here.at(ORDER[p][0]) for p in range(SLOTS)]
    m2 = [here.at(ORDER[p][1]) for p in range(SLOTS)]
    m3 = [here.at(ORDER[p][2]) for p in range(SLOTS)]
    parts = range(SLOTS)

    def to(p, axis_at, step):
        return here.to(ORDER[p][axis_at - 1], step)

    swap = copies.start(norm_ref.at[1 - c], xbuf, sib)
    other_half = pl.ds(pl.multiple_of((1 - c) * 2048, 2048), 2048)
    down_copy = copies.start(down_hbm.at[:, other_half], dsib_out, sib)
    swap.wait_recv()
    pair = pl.ds(2 * c, 2)
    for p in parts:
        mine, others = norm_ref[c, p], xbuf[p]
        low = jnp.where(c == 0, mine, others)
        high = jnp.where(c == 0, others, mine)
        rows = jnp.concatenate([low, high], axis=0).astype(BF)
        tok[2 * c, p, m3[p], m2[p], m1[p]] = rows[:, :1024]
        tok[2 * c + 1, p, m3[p], m2[p], m1[p]] = rows[:, 1024:]

    def send(region, device):
        return copies.start(region, region, device)

    first = []
    for p in parts:
        block = tok.at[pair, p, m3[p], m2[p], m1[p]]
        first.append((send(block, to(p, 1, 1)), send(block, to(p, 1, -1))))
    second = []
    for p in parts:
        for copy in first[p]:
            copy.wait_recv()
        second.append((
            send(tok.at[2 * c, p, m3[p], m2[p], mod4(m1[p] - 1)], to(p, 1, 1)),
            send(tok.at[2 * c + 1, p, m3[p], m2[p], mod4(m1[p] + 1)], to(p, 1, -1)),
        ))

    def line(p, c3, c2):
        return tok.at[pair, p, c3, c2]

    own_line = [{} for p in parts]
    ring2 = []
    subs = [[None] * 4 for p in parts]
    offsets = (0, 1, -1, 2)
    for p in parts:
        for copy in second[p]:
            copy.wait_recv()
        region = line(p, m3[p], m2[p])
        ring2.append((send(region, to(p, 2, 1)), send(region, to(p, 2, -1))))
        own_line[p][0] = send(region, sib)
    for p in parts:
        region = line(p, m3[p], m2[p])
        subs[p][0] = (send(region, to(p, 3, 1)), send(region, to(p, 3, -1)))
    ring2b = []
    for p in parts:
        for copy in ring2[p]:
            copy.wait_recv()
        ring2b.append((
            send(tok.at[2 * c, p, m3[p], mod4(m2[p] - 1)], to(p, 2, 1)),
            send(tok.at[2 * c + 1, p, m3[p], mod4(m2[p] + 1)], to(p, 2, -1)),
        ))
        for j in (1, 2):
            own_line[p][j] = send(line(p, m3[p], mod4(m2[p] + offsets[j])), sib)
    for j in (1, 2):
        for p in parts:
            region = line(p, m3[p], mod4(m2[p] + offsets[j]))
            subs[p][j] = (send(region, to(p, 3, 1)), send(region, to(p, 3, -1)))

    load_g.wait()
    load_u.wait()

    def hid_piece(p, c3, c2):
        return hid.at[p, c3, c2]

    def ffn(pieces):
        def tile(n, carry):
            cols = pl.ds(pl.multiple_of(n * 256, 256), 256)
            gate = jnp.zeros((64 * len(pieces), 256), F32)
            up = jnp.zeros((64 * len(pieces), 256), F32)
            for q in range(4):
                rows = jnp.concatenate([tok[q, p, c3, c2].reshape(64, 1024) for p, c3, c2 in pieces], axis=0)
                depth = pl.ds(q * 1024, 1024)
                gate += jnp.dot(rows, wg[depth, cols], preferred_element_type=F32)
                up += jnp.dot(rows, wu[depth, cols], preferred_element_type=F32)
            act = gate / (1.0 + jnp.exp(-gate)) * up
            for i, (p, c3, c2) in enumerate(pieces):
                weight = gw_ref[p, c3, c2][:, :1]
                hid[p, c3, c2, :, cols] = (act[64 * i : 64 * i + 64] * weight).astype(BF)
            return carry

        lax.fori_loop(0, 3, tile, 0)
        for p, c3, c2 in pieces:
            pltpu.make_async_copy(hid.at[p, c3, c2], hid_out.at[c, p, c3, c2], hloc_sem).start()
            pltpu.make_async_remote_copy(
                src_ref=hid.at[p, c3, c2],
                dst_ref=hid_out.at[c, p, c3, c2],
                send_sem=hsend_sem,
                recv_sem=hrecv_sem,
                device_id=sib,
                device_id_type=MESH,
            ).start()

    def own_unit(lines):
        for p in parts:
            for j in lines:
                own_line[p][j].wait_recv()
        ffn([(p, m3[p], mod4(m2[p] + offsets[j])) for p in parts for j in lines])

    passed = [[None] * 4 for p in parts]
    onward = [[None] * 4 for p in parts]
    opposite = [[None] * 4 for p in parts]

    def forward(j):
        for p in parts:
            line_at = mod4(m2[p] + offsets[j])
            left, right = mod4(m3[p] - 1), mod4(m3[p] + 1)
            for copy in subs[p][j]:
                copy.wait_recv()
            onward[p][j] = (
                send(tok.at[2 * c, p, left, line_at], to(p, 3, 1)),
                send(tok.at[2 * c + 1, p, right, line_at], to(p, 3, -1)),
            )
            passed[p][j] = (send(line(p, left, line_at), sib), send(line(p, right, line_at), sib))

    def near_unit(j):
        for p in parts:
            for copy in passed[p][j]:
                copy.wait_recv()
        ffn([(p, mod4(m3[p] + side), mod4(m2[p] + offsets[j])) for p in parts for side in (-1, 1)])

    def settle(j):
        for p in parts:
            for copy in onward[p][j]:
                copy.wait_recv()
            opposite[p][j] = send(line(p, mod4(m3[p] + 2), mod4(m2[p] + offsets[j])), sib)

    def far_unit(lines):
        for p in parts:
            for j in lines:
                opposite[p][j].wait_recv()
        ffn([(p, mod4(m3[p] + 2), mod4(m2[p] + offsets[j])) for p in parts for j in lines])

    own_unit((0, 1))
    for p in parts:
        for copy in ring2b[p]:
            copy.wait_recv()
        region = line(p, m3[p], mod4(m2[p] + 2))
        subs[p][3] = (send(region, to(p, 3, 1)), send(region, to(p, 3, -1)))
        own_line[p][3] = send(region, sib)
    forward(0)
    own_unit((2, 3))
    forward(1)
    near_unit(0)
    forward(2)
    settle(0)
    near_unit(1)
    forward(3)
    settle(1)
    near_unit(2)
    far_unit((0, 1))
    settle(2)
    near_unit(3)
    settle(3)
    far_unit((2, 3))

    copies.finish()
    down_copy.wait_recv()
    whole = pltpu.make_async_remote_copy(
        src_ref=hid,
        dst_ref=hid_out.at[1 - c],
        send_sem=hsend_sem,
        recv_sem=hrecv_sem,
        device_id=sib,
        device_id_type=MESH,
    )
    whole.wait_send()
    whole.wait_recv()
    pltpu.make_async_copy(hid, hid_out.at[c], hloc_sem).wait()


def expert_hidden(norm_halves, gate_weight, gate_w, up_w, down_w):
    any_space = pl.BlockSpec(memory_space=pl.ANY)
    vmem = pl.BlockSpec(memory_space=pltpu.VMEM)
    count = 2 + SLOTS * (4 + 4 + 16 + 16)
    return pl.pallas_call(
        gather_kernel,
        out_shape=(
            jax.ShapeDtypeStruct((2, SLOTS, 4, 4, 64, 768), BF),
            jax.ShapeDtypeStruct((768, 2048), BF),
        ),
        in_specs=[vmem, vmem, any_space, any_space, any_space],
        out_specs=(any_space, any_space),
        scratch_shapes=[
            pltpu.VMEM((4, SLOTS, 4, 4, 4, 16, 1024), BF),
            pltpu.VMEM((SLOTS, 8, 2048), F32),
            pltpu.VMEM((4096, 768), BF),
            pltpu.VMEM((4096, 768), BF),
            pltpu.VMEM((SLOTS, 4, 4, 64, 768), BF),
            pltpu.SemaphoreType.DMA((count,)),
            pltpu.SemaphoreType.DMA((count,)),
            pltpu.SemaphoreType.DMA((2,)),
            pltpu.SemaphoreType.DMA,
            pltpu.SemaphoreType.DMA,
            pltpu.SemaphoreType.DMA,
        ],
        compiler_params=pltpu.CompilerParams(
            collective_id=1, has_side_effects=True, vmem_limit_bytes=60 * 1024 * 1024
        ),
        name="gather_hidden",
    )(norm_halves, gate_weight, gate_w, up_w, down_w)


def scatter_kernel(
    hid_hbm, down_hbm, dsib_hbm,
    out_ref,
    hv, dw, part_sum, far3, near3, far2, near2, far1, near1, fin,
    send_sem, recv_sem, load_sem,
):
    here = Place()
    c = here.core
    sib = here.sibling()
    parts = range(SLOTS)
    m1 = [here.at(ORDER[p][0]) for p in parts]
    m2 = [here.at(ORDER[p][1]) for p in parts]
    m3 = [here.at(ORDER[p][2]) for p in parts]
    my_half = pl.ds(pl.multiple_of(c * 2048, 2048), 2048)
    loads = {}

    def load(src, dst):
        copy = pltpu.make_async_copy(src, dst, load_sem.at[len(loads)])
        copy.start()
        loads[len(loads)] = copy
        return copy

    loaded_w = [load(down_hbm.at[:, my_half], dw.at[c]), load(dsib_hbm, dw.at[1 - c])]
    planes = (2, 1, -1, 0)
    loaded_h = {}
    for off in planes:
        for p in parts:
            at = mod4(m3[p] + off)
            loaded_h[off, p] = load(hid_hbm.at[:, p, at], hv.at[:, p, at])
    here.greet(("x", "y", "z"))
    copies = Copies(send_sem, recv_sem)

    def to(p, axis_at, step):
        return here.to(ORDER[p][axis_at - 1], step)

    for copy in loaded_w:
        copy.wait()

    def down(p, off):
        at = mod4(m3[p] + off)
        loaded_h[off, p].wait()

        def tile(n, carry):
            cols = pl.ds(pl.multiple_of(n * 512, 512), 512)
            total = jnp.dot(hv[0, p, at].reshape(256, 768), dw[0, :, cols], preferred_element_type=F32)
            total += jnp.dot(hv[1, p, at].reshape(256, 768), dw[1, :, cols], preferred_element_type=F32)
            into = pl.ds(pl.multiple_of(lax.rem(n, 2) * 512, 512), 512)
            part_sum[lax.div(n, 2), p, at, :, :, into] = total.astype(BF).reshape(4, 64, 512)
            return carry

        lax.fori_loop(0, 4, tile, 0)

    def add(ref, *others):
        total = ref[...].astype(F32)
        for other in others:
            total += other[...].astype(F32)
        ref[...] = total.astype(BF)

    lines = (2, 1, -1, 0)

    def at_line(p, k):
        return mod4(m2[p] + lines[k])

    far_copy = {}
    for p in parts:
        down(p, 2)
        at = mod4(m3[p] + 2)
        for k in range(4):
            l = at_line(p, k)
            far_copy[p, k] = (
                copies.start(part_sum.at[0, p, at, l], far3.at[0, p, k], to(p, 3, 1)),
                copies.start(part_sum.at[1, p, at, l], far3.at[1, p, k], to(p, 3, -1)),
            )
    for p in parts:
        down(p, 1)
        down(p, -1)
    near_copy = {}

    def pass_near(k):
        for p in parts:
            l = at_line(p, k)
            right, left = mod4(m3[p] + 1), mod4(m3[p] - 1)
            near_copy[p, k] = [
                copies.start(part_sum.at[1, p, right, l], near3.at[0, 1, p, k], to(p, 3, 1)),
                copies.start(part_sum.at[0, p, left, l], near3.at[1, 0, p, k], to(p, 3, -1)),
            ]
            for copy in far_copy[p, k]:
                copy.wait_recv()
            add(part_sum.at[0, p, right, l], far3.at[0, p, k])
            add(part_sum.at[1, p, left, l], far3.at[1, p, k])
            near_copy[p, k] += [
                copies.start(part_sum.at[0, p, right, l], near3.at[0, 0, p, k], to(p, 3, 1)),
                copies.start(part_sum.at[1, p, left, l], near3.at[1, 1, p, k], to(p, 3, -1)),
            ]

    pass_near(0)
    for p in parts:
        down(p, 0)
    pass_near(1)
    pass_near(2)
    pass_near(3)

    def take_near(p, k):
        for copy in near_copy[p, k]:
            copy.wait_recv()
        for q in range(2):
            add(part_sum.at[q, p, m3[p], at_line(p, k)], near3.at[0, q, p, k], near3.at[1, q, p, k])

    far2_copy, near2_copy = {}, {}
    for p in parts:
        take_near(p, 0)
        l = at_line(p, 0)
        far2_copy[p] = (
            copies.start(part_sum.at[0, p, m3[p], l], far2.at[0, p], to(p, 2, 1)),
            copies.start(part_sum.at[1, p, m3[p], l], far2.at[1, p], to(p, 2, -1)),
        )
    for k, side in ((1, 0), (2, 1)):
        for p in parts:
            take_near(p, k)
            l = at_line(p, k)
            far2_copy[p][side].wait_recv()
            add(part_sum.at[side, p, m3[p], l], far2.at[side, p])
            near2_copy[p, side] = copies.start(
                part_sum.at[:, p, m3[p], l], near2.at[side, :, p], to(p, 2, 1 if side == 0 else -1)
            )
    far1_copy, near1_copy = {}, {}

    def block(p, step):
        return pl.ds(pl.multiple_of(mod4(m1[p] + step) * 16, 16), 16)

    for p in parts:
        take_near(p, 3)
        for side in range(2):
            near2_copy[p, side].wait_recv()
        for q in range(2):
            add(part_sum.at[q, p, m3[p], m2[p]], near2.at[0, q, p], near2.at[1, q, p])
        far1_copy[p] = (
            copies.start(part_sum.at[0, p, m3[p], m2[p], block(p, 2)], far1.at[0, p], to(p, 1, 1)),
            copies.start(part_sum.at[1, p, m3[p], m2[p], block(p, 2)], far1.at[1, p], to(p, 1, -1)),
        )
    for p in parts:
        for side, step in ((0, 1), (1, -1)):
            far1_copy[p][side].wait_recv()
            add(part_sum.at[side, p, m3[p], m2[p], block(p, step)], far1.at[side, p])
            near1_copy[p, side] = copies.start(
                part_sum.at[:, p, m3[p], m2[p], block(p, step)], near1.at[side, :, p], to(p, 1, step)
            )
    for p in parts:
        for side in range(2):
            near1_copy[p, side].wait_recv()
        for q in range(2):
            total = part_sum[q, p, m3[p], m2[p], block(p, 0)].astype(F32)
            total += near1[0, q, p].astype(F32) + near1[1, q, p].astype(F32)
            fin[0, p, :, q * 1024 : q * 1024 + 1024] = total[:8]
            fin[1, p, :, q * 1024 : q * 1024 + 1024] = total[8:]
    last = copies.start(fin.at[1 - c], out_ref.at[c], sib)
    out_ref[c] = fin[c]
    last.wait_recv()
    copies.finish()


def expert_sum(hidden, down_w, down_sib):
    any_space = pl.BlockSpec(memory_space=pl.ANY)
    vmem = pl.BlockSpec(memory_space=pltpu.VMEM)
    count = SLOTS * (8 + 16 + 4 + 4) + 1
    return pl.pallas_call(
        scatter_kernel,
        out_shape=jax.ShapeDtypeStruct((2, SLOTS, 8, 2048), F32),
        in_specs=[any_space, any_space, any_space],
        out_specs=vmem,
        scratch_shapes=[
            pltpu.VMEM((2, SLOTS, 4, 4, 64, 768), BF),
            pltpu.VMEM((2, 768, 2048), BF),
            pltpu.VMEM((2, SLOTS, 4, 4, 64, 1024), BF),
            pltpu.VMEM((2, SLOTS, 4, 64, 1024), BF),
            pltpu.VMEM((2, 2, SLOTS, 4, 64, 1024), BF),
            pltpu.VMEM((2, SLOTS, 64, 1024), BF),
            pltpu.VMEM((2, 2, SLOTS, 64, 1024), BF),
            pltpu.VMEM((2, SLOTS, 16, 1024), BF),
            pltpu.VMEM((2, 2, SLOTS, 16, 1024), BF),
            pltpu.VMEM((2, SLOTS, 8, 2048), F32),
            pltpu.SemaphoreType.DMA((count,)),
            pltpu.SemaphoreType.DMA((count,)),
            pltpu.SemaphoreType.DMA((14,)),
        ],
        compiler_params=pltpu.CompilerParams(
            collective_id=2, has_side_effects=True, vmem_limit_bytes=60 * 1024 * 1024
        ),
        name="down_scatter",
    )(hidden, down_w, down_sib)


def attend(packed):
    query_part = packed[..., :DH]
    key_part = packed[..., DH : 2 * DH]
    value_part = packed[..., 2 * DH :]
    scores = jnp.einsum(
        "aqhd,akhd->ahqk", query_part, key_part, preferred_element_type=jnp.float32
    ) * (1.0 / math.sqrt(DH))
    highest = jnp.max(scores, axis=-1, keepdims=True)
    raised = jnp.exp(scores - highest)
    attn_weights = (raised / jnp.sum(raised, axis=-1, keepdims=True)).astype(jnp.bfloat16)
    return jnp.einsum(
        "ahqk,akhd->aqhd", attn_weights, value_part, preferred_element_type=jnp.float32
    ).astype(jnp.bfloat16)


def on_device(
    states, query_in, key_in, value_in, cached_delta, recompute, expert_ids, expert_weights,
    norm_gain, out_proj, gate_proj, up_proj, down_proj,
):
    dev_count = lax.axis_size("dev")
    req_here, seq_here, features = states.shape
    repeat_factor = HEADS // KV_HEADS
    rank = jnp.cumsum(recompute) - 1
    live_count = jnp.sum(recompute)
    idle_rank = live_count + jnp.cumsum(1 - recompute) - 1
    place = jnp.where(recompute == 1, rank, idle_rank)
    pick = (place[None, :] == jnp.arange(SLOTS, dtype=jnp.int32)[:, None]).astype(jnp.int32)
    chosen = jnp.sum(pick * jnp.arange(req_here, dtype=jnp.int32)[None, :], axis=1)
    live_slot = jnp.arange(SLOTS, dtype=jnp.int32) < live_count

    def select(whole):
        return jnp.concatenate(
            [lax.dynamic_slice_in_dim(whole, chosen[s], 1, 0) for s in range(SLOTS)], axis=0
        )

    ids = select(expert_ids.reshape(req_here, seq_here, -1))
    weights = select(expert_weights.reshape(req_here, seq_here, -1))
    experts = jnp.arange(dev_count, dtype=jnp.int32)
    dense = jnp.sum(
        jnp.where(ids[..., None] == experts, weights[..., None], 0.0), axis=2
    )
    dense = jnp.where(live_slot[:, None, None], dense, 0.0).reshape(SLOTS * seq_here, dev_count)
    all_dense = lax.all_gather(dense, ("grp", "dev"), axis=0, tiled=False)
    mine = lax.dynamic_index_in_dim(all_dense, lax.axis_index("dev"), axis=2, keepdims=False)
    mine = mine.reshape(4, 4, 4, 2, SLOTS, seq_here)
    gate_weight = jnp.stack(
        [
            mine[:, :, :, :, 0].reshape(4, 4, 64),
            mine[:, :, :, :, 1].transpose(2, 0, 1, 3, 4).reshape(4, 4, 64),
            mine[:, :, :, :, 2].transpose(1, 2, 0, 3, 4).reshape(4, 4, 64),
        ]
    )
    gate_weight = jnp.broadcast_to(gate_weight[..., None], gate_weight.shape + (128,))

    queries = select(query_in).reshape(SLOTS, seq_here, HEADS, DH)
    keys_wide = jnp.repeat(
        select(key_in).reshape(SLOTS, seq_here, KV_HEADS, DH), repeat_factor, axis=2
    )
    values_wide = jnp.repeat(
        select(value_in).reshape(SLOTS, seq_here, KV_HEADS, DH), repeat_factor, axis=2
    )
    stacked = jnp.concatenate([queries, keys_wide, values_wide], axis=3)
    attended = attend(lax.all_to_all(stacked, "dev", split_axis=2, concat_axis=1, tiled=True))
    gathered_rows = (
        attended.reshape(SLOTS, dev_count, seq_here, DH)
        .transpose(1, 0, 2, 3)
        .reshape(dev_count * SLOTS * seq_here, DH)
    )
    projected = (
        lax.psum_scatter(
            jnp.dot(gathered_rows, out_proj, preferred_element_type=jnp.float32).astype(
                jnp.bfloat16
            ),
            "dev",
            scatter_dimension=0,
            tiled=True,
        )
        .astype(jnp.float32)
        .reshape(SLOTS, seq_here, features)
    )
    residual = select(states).astype(jnp.float32) + projected
    mean_square = jnp.mean(residual * residual, axis=-1, keepdims=True)
    normed = residual * lax.rsqrt(mean_square + 1e-06) * norm_gain
    halves = normed.reshape(SLOTS, seq_here, 2, 2048).transpose(2, 0, 1, 3)
    hidden, down_sib = expert_hidden(halves, gate_weight, gate_proj[0], up_proj[0], down_proj[0])
    moe = expert_sum(hidden, down_proj[0], down_sib)
    fresh = residual + moe.transpose(1, 2, 0, 3).reshape(SLOTS, seq_here, features)
    reused = states.astype(jnp.float32) + cached_delta.astype(jnp.float32)
    spread = sum(
        jnp.where((place == s)[:, None, None], fresh[s][None], 0.0) for s in range(SLOTS)
    )
    layer_out = jnp.where((recompute == 1)[:, None, None], spread, reused)
    return layer_out.astype(jnp.bfloat16)


def solution(mesh):
    return jax.shard_map(
        on_device,
        mesh=mesh,
        in_specs=(
            P("grp", "dev", None),
            P("grp", "dev", None),
            P("grp", "dev", None),
            P("grp", "dev", None),
            P("grp", "dev", None),
            P("grp"),
            P(("grp", "dev"), None),
            P(("grp", "dev"), None),
            P(),
            P("dev", None),
            P("dev", None, "grp"),
            P("dev", None, "grp"),
            P("dev", "grp", None),
        ),
        out_specs=P("grp", "dev", None),
        check_vma=False,
    )
```

```python
import math

import jax
import jax.numpy as jnp
from jax import lax
from jax.experimental import pallas as pl
from jax.experimental.pallas import tpu as pltpu
from jax.sharding import PartitionSpec as P

HEADS = 32
KV_HEADS = 8
DH = 128
SLOTS = 3
BF = jnp.bfloat16
F32 = jnp.float32
MESH = pl.DeviceIdType.MESH
ORDER = (("x", "z", "y"), ("z", "y", "x"), ("y", "x", "z"))


def mod4(v):
    return lax.rem(v + 4, 4)


class Place:
    def __init__(self):
        self.y = lax.axis_index("grp")
        dev = lax.axis_index("dev")
        self.core = lax.rem(dev, 2)
        self.x = lax.rem(lax.div(dev, 2), 4)
        self.z = lax.div(dev, 8)

    def at(self, axis):
        return {"x": self.x, "y": self.y, "z": self.z}[axis]

    def to(self, axis, step):
        y, x, z = self.y, self.x, self.z
        if axis == "y":
            y = mod4(y + step)
        elif axis == "x":
            x = mod4(x + step)
        else:
            z = mod4(z + step)
        return (y, (z * 4 + x) * 2 + self.core)

    def sibling(self):
        return (self.y, (self.z * 4 + self.x) * 2 + 1 - self.core)

    def greet(self, axes):
        barrier = pltpu.get_barrier_semaphore()
        others = [self.to(axis, step) for axis in axes for step in (1, -1)]
        others.append(self.sibling())
        for other in others:
            pl.semaphore_signal(barrier, inc=1, device_id=other, device_id_type=MESH)
        pl.semaphore_wait(barrier, len(others))


class Copies:
    def __init__(self, send_sem, recv_sem):
        self.send_sem, self.recv_sem = send_sem, recv_sem
        self.made = []

    def start(self, src, dst, device):
        k = len(self.made)
        copy = pltpu.make_async_remote_copy(
            src_ref=src,
            dst_ref=dst,
            send_sem=self.send_sem.at[k],
            recv_sem=self.recv_sem.at[k],
            device_id=device,
            device_id_type=MESH,
        )
        copy.start()
        self.made.append(copy)
        return copy

    def finish(self):
        for copy in self.made:
            copy.wait_send()


def gather_kernel(
    norm_ref, route_ref, gate_hbm, up_hbm, down_hbm,
    hid_out, dsib_out,
    tok, wg, wu, hid, send_sem, recv_sem, load_sem, hsend_sem, hrecv_sem, hloc_sem,
):
    here = Place()
    c = here.core
    sib = here.sibling()
    load_g = pltpu.make_async_copy(gate_hbm, wg, load_sem.at[0])
    load_u = pltpu.make_async_copy(up_hbm, wu, load_sem.at[1])
    load_g.start()
    load_u.start()
    here.greet(("x", "y", "z"))
    copies = Copies(send_sem, recv_sem)
    m1 = [here.at(ORDER[p][0]) for p in range(SLOTS)]
    m2 = [here.at(ORDER[p][1]) for p in range(SLOTS)]
    m3 = [here.at(ORDER[p][2]) for p in range(SLOTS)]
    parts = range(SLOTS)

    def to(p, axis_at, step):
        return here.to(ORDER[p][axis_at - 1], step)

    other_half = pl.ds(pl.multiple_of((1 - c) * 2048, 2048), 2048)
    down_copy = copies.start(down_hbm.at[:, other_half], dsib_out, sib)
    pair = pl.ds(2 * c, 2)
    for p in parts:
        for h in range(2):
            tok[2 * c + h, p, m3[p], m2[p], m1[p]] = norm_ref[h, p]

    def send(region, device):
        return copies.start(region, region, device)

    first = []
    for p in parts:
        block = tok.at[pair, p, m3[p], m2[p], m1[p]]
        first.append((send(block, to(p, 1, 1)), send(block, to(p, 1, -1))))
    second = []
    for p in parts:
        for copy in first[p]:
            copy.wait_recv()
        second.append((
            send(tok.at[2 * c, p, m3[p], m2[p], mod4(m1[p] - 1)], to(p, 1, 1)),
            send(tok.at[2 * c + 1, p, m3[p], m2[p], mod4(m1[p] + 1)], to(p, 1, -1)),
        ))

    def line(p, c3, c2):
        return tok.at[pair, p, c3, c2]

    own_line = [{} for p in parts]
    ring2 = []
    subs = [[None] * 4 for p in parts]
    offsets = (0, 1, -1, 2)
    for p in parts:
        for copy in second[p]:
            copy.wait_recv()
        region = line(p, m3[p], m2[p])
        ring2.append((send(region, to(p, 2, 1)), send(region, to(p, 2, -1))))
        own_line[p][0] = send(region, sib)
    for p in parts:
        region = line(p, m3[p], m2[p])
        subs[p][0] = (send(region, to(p, 3, 1)), send(region, to(p, 3, -1)))
    ring2b = []
    for p in parts:
        for copy in ring2[p]:
            copy.wait_recv()
        ring2b.append((
            send(tok.at[2 * c, p, m3[p], mod4(m2[p] - 1)], to(p, 2, 1)),
            send(tok.at[2 * c + 1, p, m3[p], mod4(m2[p] + 1)], to(p, 2, -1)),
        ))
        for j in (1, 2):
            own_line[p][j] = send(line(p, m3[p], mod4(m2[p] + offsets[j])), sib)
    for j in (1, 2):
        for p in parts:
            region = line(p, m3[p], mod4(m2[p] + offsets[j]))
            subs[p][j] = (send(region, to(p, 3, 1)), send(region, to(p, 3, -1)))

    load_g.wait()
    load_u.wait()

    def hid_piece(p, c3, c2):
        return hid.at[p, c3, c2]

    expert = lax.axis_index("dev")
    lane = lax.broadcasted_iota(jnp.int32, (64, 128), 1)

    def weight_of(p, c3, c2):
        index = ((c3, c2), (c2, slice(None), c3), (slice(None), c3, c2))[p]
        held = route_ref[index].reshape(64, 128)
        return jnp.sum(jnp.where(lane == p * 32 + expert, held, 0.0), axis=1, keepdims=True)

    def ffn(pieces):
        weights = [weight_of(*piece) for piece in pieces]

        def tile(n, carry):
            cols = pl.ds(pl.multiple_of(n * 256, 256), 256)
            gate = jnp.zeros((64 * len(pieces), 256), F32)
            up = jnp.zeros((64 * len(pieces), 256), F32)
            for q in range(4):
                rows = jnp.concatenate([tok[q, p, c3, c2].reshape(64, 1024) for p, c3, c2 in pieces], axis=0)
                depth = pl.ds(q * 1024, 1024)
                gate += jnp.dot(rows, wg[depth, cols], preferred_element_type=F32)
                up += jnp.dot(rows, wu[depth, cols], preferred_element_type=F32)
            act = gate / (1.0 + jnp.exp(-gate)) * up
            for i, (p, c3, c2) in enumerate(pieces):
                hid[p, c3, c2, :, cols] = (act[64 * i : 64 * i + 64] * weights[i]).astype(BF)
            return carry

        lax.fori_loop(0, 3, tile, 0)
        for p, c3, c2 in pieces:
            pltpu.make_async_copy(hid.at[p, c3, c2], hid_out.at[c, p, c3, c2], hloc_sem).start()
            pltpu.make_async_remote_copy(
                src_ref=hid.at[p, c3, c2],
                dst_ref=hid_out.at[c, p, c3, c2],
                send_sem=hsend_sem,
                recv_sem=hrecv_sem,
                device_id=sib,
                device_id_type=MESH,
            ).start()

    def own_unit(lines):
        for p in parts:
            for j in lines:
                own_line[p][j].wait_recv()
        ffn([(p, m3[p], mod4(m2[p] + offsets[j])) for p in parts for j in lines])

    passed = [[None] * 4 for p in parts]
    onward = [[None] * 4 for p in parts]
    opposite = [[None] * 4 for p in parts]

    def forward(j):
        for p in parts:
            line_at = mod4(m2[p] + offsets[j])
            left, right = mod4(m3[p] - 1), mod4(m3[p] + 1)
            for copy in subs[p][j]:
                copy.wait_recv()
            onward[p][j] = (
                send(tok.at[2 * c, p, left, line_at], to(p, 3, 1)),
                send(tok.at[2 * c + 1, p, right, line_at], to(p, 3, -1)),
            )
            passed[p][j] = (send(line(p, left, line_at), sib), send(line(p, right, line_at), sib))

    def near_unit(j):
        for p in parts:
            for copy in passed[p][j]:
                copy.wait_recv()
        ffn([(p, mod4(m3[p] + side), mod4(m2[p] + offsets[j])) for p in parts for side in (-1, 1)])

    def settle(j):
        for p in parts:
            for copy in onward[p][j]:
                copy.wait_recv()
            opposite[p][j] = send(line(p, mod4(m3[p] + 2), mod4(m2[p] + offsets[j])), sib)

    def far_unit(lines):
        for p in parts:
            for j in lines:
                opposite[p][j].wait_recv()
        ffn([(p, mod4(m3[p] + 2), mod4(m2[p] + offsets[j])) for p in parts for j in lines])

    own_unit((0, 1))
    for p in parts:
        for copy in ring2b[p]:
            copy.wait_recv()
        region = line(p, m3[p], mod4(m2[p] + 2))
        subs[p][3] = (send(region, to(p, 3, 1)), send(region, to(p, 3, -1)))
        own_line[p][3] = send(region, sib)
    forward(0)
    own_unit((2, 3))
    forward(1)
    near_unit(0)
    forward(2)
    settle(0)
    near_unit(1)
    forward(3)
    settle(1)
    near_unit(2)
    far_unit((0, 1))
    settle(2)
    near_unit(3)
    settle(3)
    far_unit((2, 3))

    copies.finish()
    down_copy.wait_recv()
    whole = pltpu.make_async_remote_copy(
        src_ref=hid,
        dst_ref=hid_out.at[1 - c],
        send_sem=hsend_sem,
        recv_sem=hrecv_sem,
        device_id=sib,
        device_id_type=MESH,
    )
    whole.wait_send()
    whole.wait_recv()
    pltpu.make_async_copy(hid, hid_out.at[c], hloc_sem).wait()


def expert_hidden(normed, route, gate_w, up_w, down_w):
    any_space = pl.BlockSpec(memory_space=pl.ANY)
    vmem = pl.BlockSpec(memory_space=pltpu.VMEM)
    count = 1 + SLOTS * (4 + 4 + 16 + 16)
    return pl.pallas_call(
        gather_kernel,
        out_shape=(
            jax.ShapeDtypeStruct((2, SLOTS, 4, 4, 64, 768), BF),
            jax.ShapeDtypeStruct((768, 2048), BF),
        ),
        in_specs=[vmem, vmem, any_space, any_space, any_space],
        out_specs=(any_space, any_space),
        scratch_shapes=[
            pltpu.VMEM((4, SLOTS, 4, 4, 4, 16, 1024), BF),
            pltpu.VMEM((4096, 768), BF),
            pltpu.VMEM((4096, 768), BF),
            pltpu.VMEM((SLOTS, 4, 4, 64, 768), BF),
            pltpu.SemaphoreType.DMA((count,)),
            pltpu.SemaphoreType.DMA((count,)),
            pltpu.SemaphoreType.DMA((2,)),
            pltpu.SemaphoreType.DMA,
            pltpu.SemaphoreType.DMA,
            pltpu.SemaphoreType.DMA,
        ],
        compiler_params=pltpu.CompilerParams(
            collective_id=1, has_side_effects=True, vmem_limit_bytes=60 * 1024 * 1024
        ),
        name="gather_hidden",
    )(normed, route, gate_w, up_w, down_w)


def scatter_kernel(
    hid_hbm, down_hbm, dsib_hbm, res_ref,
    out_ref,
    hv, dw, part_sum, far3, near3, far2, near2, far1, near1, fin,
    send_sem, recv_sem, load_sem,
):
    here = Place()
    c = here.core
    sib = here.sibling()
    parts = range(SLOTS)
    m1 = [here.at(ORDER[p][0]) for p in parts]
    m2 = [here.at(ORDER[p][1]) for p in parts]
    m3 = [here.at(ORDER[p][2]) for p in parts]
    my_half = pl.ds(pl.multiple_of(c * 2048, 2048), 2048)
    loads = {}

    def load(src, dst):
        copy = pltpu.make_async_copy(src, dst, load_sem.at[len(loads)])
        copy.start()
        loads[len(loads)] = copy
        return copy

    loaded_w = [load(down_hbm.at[:, my_half], dw.at[c]), load(dsib_hbm, dw.at[1 - c])]
    planes = (2, 1, -1, 0)
    loaded_h = {}
    for off in planes:
        for p in parts:
            at = mod4(m3[p] + off)
            loaded_h[off, p] = load(hid_hbm.at[:, p, at], hv.at[:, p, at])
    here.greet(("x", "y", "z"))
    copies = Copies(send_sem, recv_sem)

    def to(p, axis_at, step):
        return here.to(ORDER[p][axis_at - 1], step)

    for copy in loaded_w:
        copy.wait()

    def down(p, off):
        at = mod4(m3[p] + off)
        loaded_h[off, p].wait()

        def tile(n, carry):
            cols = pl.ds(pl.multiple_of(n * 512, 512), 512)
            total = jnp.dot(hv[0, p, at].reshape(256, 768), dw[0, :, cols], preferred_element_type=F32)
            total += jnp.dot(hv[1, p, at].reshape(256, 768), dw[1, :, cols], preferred_element_type=F32)
            into = pl.ds(pl.multiple_of(lax.rem(n, 2) * 512, 512), 512)
            part_sum[lax.div(n, 2), p, at, :, :, into] = total.astype(BF).reshape(4, 64, 512)
            return carry

        lax.fori_loop(0, 4, tile, 0)

    def add(ref, *others):
        total = ref[...].astype(F32)
        for other in others:
            total += other[...].astype(F32)
        ref[...] = total.astype(BF)

    lines = (2, 1, -1, 0)

    def at_line(p, k):
        return mod4(m2[p] + lines[k])

    far_copy = {}
    for p in parts:
        down(p, 2)
        at = mod4(m3[p] + 2)
        for k in range(4):
            l = at_line(p, k)
            far_copy[p, k] = (
                copies.start(part_sum.at[0, p, at, l], far3.at[0, p, k], to(p, 3, 1)),
                copies.start(part_sum.at[1, p, at, l], far3.at[1, p, k], to(p, 3, -1)),
            )
    for p in parts:
        down(p, 1)
        down(p, -1)
    near_copy = {}

    def pass_near(k):
        for p in parts:
            l = at_line(p, k)
            right, left = mod4(m3[p] + 1), mod4(m3[p] - 1)
            near_copy[p, k] = [
                copies.start(part_sum.at[1, p, right, l], near3.at[0, 1, p, k], to(p, 3, 1)),
                copies.start(part_sum.at[0, p, left, l], near3.at[1, 0, p, k], to(p, 3, -1)),
            ]
            for copy in far_copy[p, k]:
                copy.wait_recv()
            add(part_sum.at[0, p, right, l], far3.at[0, p, k])
            add(part_sum.at[1, p, left, l], far3.at[1, p, k])
            near_copy[p, k] += [
                copies.start(part_sum.at[0, p, right, l], near3.at[0, 0, p, k], to(p, 3, 1)),
                copies.start(part_sum.at[1, p, left, l], near3.at[1, 1, p, k], to(p, 3, -1)),
            ]

    pass_near(0)
    for p in parts:
        down(p, 0)
    pass_near(1)
    pass_near(2)
    pass_near(3)

    def take_near(p, k):
        for copy in near_copy[p, k]:
            copy.wait_recv()
        for q in range(2):
            add(part_sum.at[q, p, m3[p], at_line(p, k)], near3.at[0, q, p, k], near3.at[1, q, p, k])

    far2_copy, near2_copy = {}, {}
    for p in parts:
        take_near(p, 0)
        l = at_line(p, 0)
        far2_copy[p] = (
            copies.start(part_sum.at[0, p, m3[p], l], far2.at[0, p], to(p, 2, 1)),
            copies.start(part_sum.at[1, p, m3[p], l], far2.at[1, p], to(p, 2, -1)),
        )
    for k, side in ((1, 0), (2, 1)):
        for p in parts:
            take_near(p, k)
            l = at_line(p, k)
            far2_copy[p][side].wait_recv()
            add(part_sum.at[side, p, m3[p], l], far2.at[side, p])
            near2_copy[p, side] = copies.start(
                part_sum.at[:, p, m3[p], l], near2.at[side, :, p], to(p, 2, 1 if side == 0 else -1)
            )
    far1_copy, near1_copy = {}, {}

    def block(p, step):
        return pl.ds(pl.multiple_of(mod4(m1[p] + step) * 16, 16), 16)

    for p in parts:
        take_near(p, 3)
        for side in range(2):
            near2_copy[p, side].wait_recv()
        for q in range(2):
            add(part_sum.at[q, p, m3[p], m2[p]], near2.at[0, q, p], near2.at[1, q, p])
        far1_copy[p] = (
            copies.start(part_sum.at[0, p, m3[p], m2[p], block(p, 2)], far1.at[0, p], to(p, 1, 1)),
            copies.start(part_sum.at[1, p, m3[p], m2[p], block(p, 2)], far1.at[1, p], to(p, 1, -1)),
        )
    for p in parts:
        for side, step in ((0, 1), (1, -1)):
            far1_copy[p][side].wait_recv()
            add(part_sum.at[side, p, m3[p], m2[p], block(p, step)], far1.at[side, p])
            near1_copy[p, side] = copies.start(
                part_sum.at[:, p, m3[p], m2[p], block(p, step)], near1.at[side, :, p], to(p, 1, step)
            )
    for p in parts:
        for side in range(2):
            near1_copy[p, side].wait_recv()
        for q in range(2):
            total = part_sum[q, p, m3[p], m2[p], block(p, 0)].astype(F32)
            total += near1[0, q, p].astype(F32) + near1[1, q, p].astype(F32)
            total += res_ref[p, :, q * 1024 : q * 1024 + 1024]
            fin[0, p, :, q * 1024 : q * 1024 + 1024] = total[:8]
            fin[1, p, :, q * 1024 : q * 1024 + 1024] = total[8:]
    last = copies.start(fin.at[1 - c], out_ref.at[c], sib)
    out_ref[c] = fin[c]
    last.wait_recv()
    copies.finish()


def expert_sum(hidden, down_w, down_sib, residual):
    any_space = pl.BlockSpec(memory_space=pl.ANY)
    vmem = pl.BlockSpec(memory_space=pltpu.VMEM)
    count = SLOTS * (8 + 16 + 4 + 4) + 1
    return pl.pallas_call(
        scatter_kernel,
        out_shape=jax.ShapeDtypeStruct((2, SLOTS, 8, 2048), F32),
        in_specs=[any_space, any_space, any_space, vmem],
        out_specs=vmem,
        scratch_shapes=[
            pltpu.VMEM((2, SLOTS, 4, 4, 64, 768), BF),
            pltpu.VMEM((2, 768, 2048), BF),
            pltpu.VMEM((2, SLOTS, 4, 4, 64, 1024), BF),
            pltpu.VMEM((2, SLOTS, 4, 64, 1024), BF),
            pltpu.VMEM((2, 2, SLOTS, 4, 64, 1024), BF),
            pltpu.VMEM((2, SLOTS, 64, 1024), BF),
            pltpu.VMEM((2, 2, SLOTS, 64, 1024), BF),
            pltpu.VMEM((2, SLOTS, 16, 1024), BF),
            pltpu.VMEM((2, 2, SLOTS, 16, 1024), BF),
            pltpu.VMEM((2, SLOTS, 8, 2048), F32),
            pltpu.SemaphoreType.DMA((count,)),
            pltpu.SemaphoreType.DMA((count,)),
            pltpu.SemaphoreType.DMA((14,)),
        ],
        compiler_params=pltpu.CompilerParams(
            collective_id=2, has_side_effects=True, vmem_limit_bytes=60 * 1024 * 1024
        ),
        name="down_scatter",
    )(hidden, down_w, down_sib, residual)


def attend(q, k, v):
    scores = lax.dot_general(q, k, (((1,), (1,)), ((), ())), preferred_element_type=F32)
    scores = scores * (1.0 / math.sqrt(DH))
    raised = jnp.exp(scores - jnp.max(scores, axis=-1, keepdims=True))
    weights = (raised / jnp.sum(raised, axis=-1, keepdims=True)).astype(BF)
    return jnp.dot(weights, v, preferred_element_type=F32)


def attention_kernel(
    msg, route_ref, state_ref, gain_ref, proj_hbm,
    norm_out, res_out, route_out,
    got, mixed, ow, sib_state, part_sum, far_a, near_a, far_b, near_b, squares,
    send_sem, recv_sem, load_sem,
):
    here = Place()
    c = here.core
    sib = here.sibling()
    chip = here.z * 4 + here.x

    my_half = pl.ds(pl.multiple_of(c * 2048, 2048), 2048)
    other_half = pl.ds(pl.multiple_of((1 - c) * 2048, 2048), 2048)
    my_rows = pl.ds(pl.multiple_of(c * DH, DH), DH)
    load = pltpu.make_async_copy(proj_hbm.at[:, my_half], ow.at[my_rows], load_sem)
    load.start()

    hops = [(dz, dx) for dz in range(4) for dx in range(4) if (dz, dx) != (0, 0)]
    hops.sort(key=lambda hop: -(min(hop[0], 4 - hop[0]) + min(hop[1], 4 - hop[1])))

    def chip_at(dz, dx):
        return lax.rem(here.z + dz, 4) * 4 + lax.rem(here.x + dx, 4)

    barrier = pltpu.get_barrier_semaphore()
    others = [(here.y, chip_at(dz, dx) * 2 + c) for dz, dx in hops]
    greeted = others + [here.to("y", 1), here.to("y", -1), sib]
    for other in greeted:
        pl.semaphore_signal(barrier, inc=1, device_id=other, device_id_type=MESH)
    pl.semaphore_wait(barrier, len(greeted))

    copies = Copies(send_sem, recv_sem)
    arriving = []
    for (dz, dx), other in zip(hops, others):
        arriving.append(copies.start(msg.at[chip_at(dz, dx)], got.at[c, chip], other))
    got[c, chip] = msg[chip]
    route_out[here.y, here.z, here.x, c] = route_ref[...]
    tile = route_out.at[here.y, here.z, here.x, c]
    route_swap = copies.start(tile, tile, sib)
    proj_copy = copies.start(proj_hbm.at[:, other_half], ow.at[my_rows], sib)
    state_copy = copies.start(state_ref.at[1 - c], sib_state, sib)

    def ring(region, axis):
        return (copies.start(region, region, here.to(axis, 1)), copies.start(region, region, here.to(axis, -1)))

    route_swap.wait_recv()
    along_x = ring(route_out.at[here.y, here.z, here.x], "x")
    for copy in arriving:
        copy.wait_recv()
    passed = copies.start(got.at[c], got.at[c], sib)
    for copy in along_x:
        copy.wait_recv()
    left = route_out.at[here.y, here.z, mod4(here.x - 1)]
    far_x = copies.start(left, left, here.to("x", 1))
    passed.wait_recv()
    for s in range(SLOTS):
        held = got[:, :, s].astype(F32)
        q = jnp.where(c == 0, held[:, :, 0, :8], held[:, :, 0, 8:]).reshape(256, DH).astype(BF)
        k = held[:, :, 1, :8].reshape(256, DH).astype(BF)
        v = held[:, :, 1, 8:].reshape(256, DH).astype(BF)
        out = attend(q, k, v).reshape(2, 4, 4, 8, DH)
        mixed[c, :, :, s] = jnp.concatenate([out[0], out[1]], axis=2).astype(BF)
    mixed_copy = copies.start(mixed.at[c], mixed.at[c], sib)
    far_x.wait_recv()
    along_z = ring(route_out.at[here.y, here.z], "z")
    load.wait()
    proj_copy.wait_recv()
    mixed_copy.wait_recv()

    axes = (("z", "x"), ("x", "z"))
    m2 = [here.at(axes[t][0]) for t in range(2)]
    m1 = [here.at(axes[t][1]) for t in range(2)]

    def project(t, off):
        at = mod4(m2[t] + off)
        rows = [(mixed[h, at] if t == 0 else mixed[h, :, at]).reshape(192, DH) for h in range(2)]
        rows = jnp.concatenate(rows, axis=1)
        for half in range(2):
            first = t * 1024 + half * 512
            total = jnp.dot(rows, ow[:, first : first + 512], preferred_element_type=F32)
            part_sum[half, t, at] = total.astype(BF).reshape(4, 48, 512)

    def add(ref, *terms):
        total = ref[...].astype(F32)
        for term in terms:
            total += term[...].astype(F32)
        ref[...] = total.astype(BF)

    lines = (2, 1, -1, 0)
    far_copy, near_copy = {}, {}
    for t in range(2):
        project(t, 2)
        at = mod4(m2[t] + 2)
        for k in range(4):
            l = mod4(m1[t] + lines[k])
            far_copy[t, k] = (
                copies.start(part_sum.at[0, t, at, l], far_a.at[0, t, k], here.to(axes[t][0], 1)),
                copies.start(part_sum.at[1, t, at, l], far_a.at[1, t, k], here.to(axes[t][0], -1)),
            )
    for t in range(2):
        project(t, 1)
        project(t, -1)
    for k in range(4):
        for t in range(2):
            l = mod4(m1[t] + lines[k])
            right, left = mod4(m2[t] + 1), mod4(m2[t] - 1)
            to_right, to_left = here.to(axes[t][0], 1), here.to(axes[t][0], -1)
            near_copy[t, k] = [
                copies.start(part_sum.at[1, t, right, l], near_a.at[0, 1, t, k], to_right),
                copies.start(part_sum.at[0, t, left, l], near_a.at[1, 0, t, k], to_left),
            ]
            for copy in far_copy[t, k]:
                copy.wait_recv()
            add(part_sum.at[0, t, right, l], far_a.at[0, t, k])
            add(part_sum.at[1, t, left, l], far_a.at[1, t, k])
            near_copy[t, k] += [
                copies.start(part_sum.at[0, t, right, l], near_a.at[0, 0, t, k], to_right),
                copies.start(part_sum.at[1, t, left, l], near_a.at[1, 1, t, k], to_left),
            ]
        if k == 0:
            for t in range(2):
                project(t, 0)
            for copy in along_z:
                copy.wait_recv()
            behind = route_out.at[here.y, mod4(here.z - 1)]
            far_z = copies.start(behind, behind, here.to("z", 1))

    far_z.wait_recv()
    along_y = ring(route_out.at[here.y], "y")

    def take_near(t, k):
        for copy in near_copy[t, k]:
            copy.wait_recv()
        l = mod4(m1[t] + lines[k])
        for half in range(2):
            add(part_sum.at[half, t, m2[t], l], near_a.at[0, half, t, k], near_a.at[1, half, t, k])

    far_b_copy, near_b_copy = {}, {}
    for t in range(2):
        take_near(t, 0)
        l = mod4(m1[t] + 2)
        far_b_copy[t] = (
            copies.start(part_sum.at[0, t, m2[t], l], far_b.at[0, t], here.to(axes[t][1], 1)),
            copies.start(part_sum.at[1, t, m2[t], l], far_b.at[1, t], here.to(axes[t][1], -1)),
        )
    for k, side, step in ((1, 0, 1), (2, 1, -1)):
        for t in range(2):
            take_near(t, k)
            l = mod4(m1[t] + step)
            far_b_copy[t][side].wait_recv()
            add(part_sum.at[side, t, m2[t], l], far_b.at[side, t])
            near_b_copy[t, side] = copies.start(
                part_sum.at[:, t, m2[t], l], near_b.at[side, :, t], here.to(axes[t][1], step)
            )
    for copy in along_y:
        copy.wait_recv()
    behind = route_out.at[mod4(here.y - 1)]
    far_y = copies.start(behind, behind, here.to("y", 1))
    state_copy.wait_recv()
    square = jnp.zeros((48, 1), F32)
    for t in range(2):
        for copy in near_copy[t, 3]:
            copy.wait_recv()
        for side in range(2):
            near_b_copy[t, side].wait_recv()
        for half in range(2):
            total = part_sum[half, t, m2[t], m1[t]].astype(F32)
            for side in range(2):
                total += near_a[side, half, t, 3].astype(F32)
            for side in range(2):
                total += near_b[side, half, t].astype(F32)
            first = t * 1024 + half * 512
            cols = slice(first, first + 512)
            mine = state_ref[c, :, :, cols]
            theirs = sib_state[:, :, cols]
            low = jnp.where(c == 0, mine, theirs)
            high = jnp.where(c == 0, theirs, mine)
            total += jnp.concatenate([low, high], axis=1).reshape(48, 512)
            res_out[:, :, cols] = total.reshape(SLOTS, 16, 512)
            square += jnp.sum(total * total, axis=1, keepdims=True)
    squares[c] = jnp.broadcast_to(square, (48, 128))
    square_copy = copies.start(squares.at[c], squares.at[c], sib)
    square_copy.wait_recv()
    mean = (squares[0, :, :1] + squares[1, :, :1]) * (1.0 / 4096.0)
    factor = lax.rsqrt(mean + 1e-06).reshape(SLOTS, 16, 1)
    for h in range(2):
        cols = slice(h * 1024, h * 1024 + 1024)
        gain = gain_ref[pl.ds(c, 1), cols].reshape(1, 1, 1024)
        norm_out[h] = (res_out[:, :, cols] * factor * gain).astype(BF)
    far_y.wait_recv()
    copies.finish()


def attention(msg, route, state, gain, out_proj):
    any_space = pl.BlockSpec(memory_space=pl.ANY)
    vmem = pl.BlockSpec(memory_space=pltpu.VMEM)
    count = 15 + 1 + 1 + 1 + 1 + 1 + 2 * (8 + 16 + 2 + 2) + 9 + 1
    return pl.pallas_call(
        attention_kernel,
        out_shape=(
            jax.ShapeDtypeStruct((2, SLOTS, 16, 1024), BF),
            jax.ShapeDtypeStruct((SLOTS, 16, 2048), F32),
            jax.ShapeDtypeStruct((4, 4, 4, 2, 8, 128), F32),
        ),
        in_specs=[vmem, vmem, vmem, vmem, any_space],
        out_specs=(vmem, vmem, vmem),
        scratch_shapes=[
            pltpu.VMEM((2, 16, SLOTS, 2, 16, DH), BF),
            pltpu.VMEM((2, 4, 4, SLOTS, 16, DH), BF),
            pltpu.VMEM((2 * DH, 2048), BF),
            pltpu.VMEM((SLOTS, 8, 2048), F32),
            pltpu.VMEM((2, 2, 4, 4, 48, 512), BF),
            pltpu.VMEM((2, 2, 4, 48, 512), BF),
            pltpu.VMEM((2, 2, 2, 4, 48, 512), BF),
            pltpu.VMEM((2, 2, 48, 512), BF),
            pltpu.VMEM((2, 2, 2, 48, 512), BF),
            pltpu.VMEM((2, 48, 128), F32),
            pltpu.SemaphoreType.DMA((count,)),
            pltpu.SemaphoreType.DMA((count,)),
            pltpu.SemaphoreType.DMA,
        ],
        compiler_params=pltpu.CompilerParams(
            collective_id=3, has_side_effects=True, vmem_limit_bytes=48 * 1024 * 1024
        ),
        name="attention_norm",
    )(msg, route, state, gain, out_proj)


def on_device(
    states, query_in, key_in, value_in, cached_delta, recompute, expert_ids, expert_weights,
    norm_gain, out_proj, gate_proj, up_proj, down_proj,
):
    dev_count = lax.axis_size("dev")
    req_here, seq_here, features = states.shape
    rank = jnp.cumsum(recompute) - 1
    live_count = jnp.sum(recompute)
    idle_rank = live_count + jnp.cumsum(1 - recompute) - 1
    place = jnp.where(recompute == 1, rank, idle_rank)
    pick = (place[None, :] == jnp.arange(SLOTS, dtype=jnp.int32)[:, None]).astype(jnp.int32)
    chosen = jnp.sum(pick * jnp.arange(req_here, dtype=jnp.int32)[None, :], axis=1)
    live_slot = jnp.arange(SLOTS, dtype=jnp.int32) < live_count

    def select(whole):
        return jnp.concatenate(
            [lax.dynamic_slice_in_dim(whole, chosen[s], 1, 0) for s in range(SLOTS)], axis=0
        )

    ids = select(expert_ids.reshape(req_here, seq_here, -1))
    weights = select(expert_weights.reshape(req_here, seq_here, -1))
    experts = jnp.arange(dev_count, dtype=jnp.int32)
    dense = jnp.sum(
        jnp.where(ids[..., None] == experts, weights[..., None], 0.0), axis=2
    )
    dense = jnp.where(live_slot[:, None, None], dense, 0.0)
    route = dense.transpose(1, 0, 2).reshape(seq_here, -1)
    route = jnp.pad(route, ((0, 0), (0, 128 - SLOTS * dev_count)))

    chips = dev_count // 2
    queries = select(query_in).reshape(SLOTS, seq_here, chips, 2, DH).transpose(2, 0, 3, 1, 4)
    keys = select(key_in).reshape(SLOTS, seq_here, KV_HEADS, DH)
    values = select(value_in).reshape(SLOTS, seq_here, KV_HEADS, DH)
    both = jnp.stack([keys, values]).transpose(3, 1, 0, 2, 4)
    both = jnp.repeat(both, chips // KV_HEADS, axis=0)
    msg = jnp.stack(
        [queries.reshape(chips, SLOTS, 16, DH), both.reshape(chips, SLOTS, 16, DH)], axis=2
    )
    state = select(states).astype(F32).reshape(SLOTS, seq_here, 2, 2048).transpose(2, 0, 1, 3)
    normed, residual, routes = attention(msg, route, state, norm_gain.reshape(2, 2048), out_proj)
    hidden, down_sib = expert_hidden(normed, routes, gate_proj[0], up_proj[0], down_proj[0])
    fresh = expert_sum(hidden, down_proj[0], down_sib, residual)
    fresh = fresh.transpose(1, 2, 0, 3).reshape(SLOTS, seq_here, features)
    reused = states.astype(jnp.float32) + cached_delta.astype(jnp.float32)
    spread = sum(
        jnp.where((place == s)[:, None, None], fresh[s][None], 0.0) for s in range(SLOTS)
    )
    layer_out = jnp.where((recompute == 1)[:, None, None], spread, reused)
    return layer_out.astype(jnp.bfloat16)


def solution(mesh):
    return jax.shard_map(
        on_device,
        mesh=mesh,
        in_specs=(
            P("grp", "dev", None),
            P("grp", "dev", None),
            P("grp", "dev", None),
            P("grp", "dev", None),
            P("grp", "dev", None),
            P("grp"),
            P(("grp", "dev"), None),
            P(("grp", "dev"), None),
            P(),
            P("dev", None),
            P("dev", None, "grp"),
            P("dev", None, "grp"),
            P("dev", "grp", None),
        ),
        out_specs=P("grp", "dev", None),
        check_vma=False,
    )
```

```python
import math

import jax
import jax.numpy as jnp
from jax import lax
from jax.experimental import pallas as pl
from jax.experimental.pallas import tpu as pltpu
from jax.sharding import PartitionSpec as P

HEADS = 32
KV_HEADS = 8
DH = 128
SLOTS = 3
BF = jnp.bfloat16
F32 = jnp.float32
MESH = pl.DeviceIdType.MESH
ORDER = (("x", "z", "y"), ("z", "y", "x"), ("y", "x", "z"))


def mod4(v):
    return lax.rem(v + 4, 4)


class Place:
    def __init__(self):
        self.y = lax.axis_index("grp")
        dev = lax.axis_index("dev")
        self.core = lax.rem(dev, 2)
        self.x = lax.rem(lax.div(dev, 2), 4)
        self.z = lax.div(dev, 8)

    def at(self, axis):
        return {"x": self.x, "y": self.y, "z": self.z}[axis]

    def to(self, axis, step):
        y, x, z = self.y, self.x, self.z
        if axis == "y":
            y = mod4(y + step)
        elif axis == "x":
            x = mod4(x + step)
        else:
            z = mod4(z + step)
        return (y, (z * 4 + x) * 2 + self.core)

    def sibling(self):
        return (self.y, (self.z * 4 + self.x) * 2 + 1 - self.core)

    def greet(self, axes):
        barrier = pltpu.get_barrier_semaphore()
        others = [self.to(axis, step) for axis in axes for step in (1, -1)]
        others.append(self.sibling())
        for other in others:
            pl.semaphore_signal(barrier, inc=1, device_id=other, device_id_type=MESH)
        pl.semaphore_wait(barrier, len(others))


class Copies:
    def __init__(self, send_sem, recv_sem):
        self.send_sem, self.recv_sem = send_sem, recv_sem
        self.made = []

    def start(self, src, dst, device):
        k = len(self.made)
        copy = pltpu.make_async_remote_copy(
            src_ref=src,
            dst_ref=dst,
            send_sem=self.send_sem.at[k],
            recv_sem=self.recv_sem.at[k],
            device_id=device,
            device_id_type=MESH,
        )
        copy.start()
        self.made.append(copy)
        return copy

    def finish(self):
        for copy in self.made:
            copy.wait_send()


def gather_kernel(
    norm_ref, route_ref, gate_hbm, up_hbm, down_hbm,
    hid_out, dsib_out,
    tok, wg, wu, hid, send_sem, recv_sem, load_sem, hsend_sem, hrecv_sem, hloc_sem,
):
    here = Place()
    c = here.core
    sib = here.sibling()
    load_g = pltpu.make_async_copy(gate_hbm, wg, load_sem.at[0])
    load_u = pltpu.make_async_copy(up_hbm, wu, load_sem.at[1])
    load_g.start()
    load_u.start()
    here.greet(("x", "y", "z"))
    copies = Copies(send_sem, recv_sem)
    m1 = [here.at(ORDER[p][0]) for p in range(SLOTS)]
    m2 = [here.at(ORDER[p][1]) for p in range(SLOTS)]
    m3 = [here.at(ORDER[p][2]) for p in range(SLOTS)]
    parts = range(SLOTS)

    def to(p, axis_at, step):
        return here.to(ORDER[p][axis_at - 1], step)

    other_half = pl.ds(pl.multiple_of((1 - c) * 2048, 2048), 2048)
    pair = pl.ds(2 * c, 2)
    for p in parts:
        for h in range(2):
            tok[2 * c + h, p, m3[p], m2[p], m1[p]] = norm_ref[h, p]

    def send(region, device):
        return copies.start(region, region, device)

    first = []
    for p in parts:
        block = tok.at[pair, p, m3[p], m2[p], m1[p]]
        first.append((send(block, to(p, 1, 1)), send(block, to(p, 1, -1))))
    second = []
    for p in parts:
        for copy in first[p]:
            copy.wait_recv()
        second.append((
            send(tok.at[2 * c, p, m3[p], m2[p], mod4(m1[p] - 1)], to(p, 1, 1)),
            send(tok.at[2 * c + 1, p, m3[p], m2[p], mod4(m1[p] + 1)], to(p, 1, -1)),
        ))

    def line(p, c3, c2):
        return tok.at[pair, p, c3, c2]

    own_line = [{} for p in parts]
    ring2 = []
    subs = [[None] * 4 for p in parts]
    offsets = (0, 1, -1, 2)
    for p in parts:
        for copy in second[p]:
            copy.wait_recv()
        region = line(p, m3[p], m2[p])
        ring2.append((send(region, to(p, 2, 1)), send(region, to(p, 2, -1))))
        own_line[p][0] = send(region, sib)
    for p in parts:
        region = line(p, m3[p], m2[p])
        subs[p][0] = (send(region, to(p, 3, 1)), send(region, to(p, 3, -1)))
    ring2b = []
    for p in parts:
        for copy in ring2[p]:
            copy.wait_recv()
        ring2b.append((
            send(tok.at[2 * c, p, m3[p], mod4(m2[p] - 1)], to(p, 2, 1)),
            send(tok.at[2 * c + 1, p, m3[p], mod4(m2[p] + 1)], to(p, 2, -1)),
        ))
        for j in (1, 2):
            own_line[p][j] = send(line(p, m3[p], mod4(m2[p] + offsets[j])), sib)
    for j in (1, 2):
        for p in parts:
            region = line(p, m3[p], mod4(m2[p] + offsets[j]))
            subs[p][j] = (send(region, to(p, 3, 1)), send(region, to(p, 3, -1)))

    load_g.wait()
    load_u.wait()

    def hid_piece(p, c3, c2):
        return hid.at[p, c3, c2]

    expert = lax.axis_index("dev")
    lane = lax.broadcasted_iota(jnp.int32, (64, 128), 1)

    def weight_of(p, c3, c2):
        index = ((c3, c2), (c2, slice(None), c3), (slice(None), c3, c2))[p]
        held = route_ref[index].reshape(64, 128)
        return jnp.sum(jnp.where(lane == p * 32 + expert, held, 0.0), axis=1, keepdims=True)

    def ffn(pieces):
        weights = [weight_of(*piece) for piece in pieces]

        def tile(n, carry):
            cols = pl.ds(pl.multiple_of(n * 256, 256), 256)
            gate = jnp.zeros((64 * len(pieces), 256), F32)
            up = jnp.zeros((64 * len(pieces), 256), F32)
            for q in range(4):
                rows = jnp.concatenate([tok[q, p, c3, c2].reshape(64, 1024) for p, c3, c2 in pieces], axis=0)
                depth = pl.ds(q * 1024, 1024)
                gate += jnp.dot(rows, wg[depth, cols], preferred_element_type=F32)
                up += jnp.dot(rows, wu[depth, cols], preferred_element_type=F32)
            act = gate / (1.0 + jnp.exp(-gate)) * up
            for i, (p, c3, c2) in enumerate(pieces):
                hid[p, c3, c2, :, cols] = (act[64 * i : 64 * i + 64] * weights[i]).astype(BF)
            return carry

        lax.fori_loop(0, 3, tile, 0)
        for p, c3, c2 in pieces:
            pltpu.make_async_copy(hid.at[p, c3, c2], hid_out.at[c, p, c3, c2], hloc_sem).start()
            pltpu.make_async_remote_copy(
                src_ref=hid.at[p, c3, c2],
                dst_ref=hid_out.at[c, p, c3, c2],
                send_sem=hsend_sem,
                recv_sem=hrecv_sem,
                device_id=sib,
                device_id_type=MESH,
            ).start()

    def own_unit(lines):
        for p in parts:
            for j in lines:
                own_line[p][j].wait_recv()
        ffn([(p, m3[p], mod4(m2[p] + offsets[j])) for p in parts for j in lines])

    passed = [[None] * 4 for p in parts]
    onward = [[None] * 4 for p in parts]
    opposite = [[None] * 4 for p in parts]

    def forward(j):
        for p in parts:
            line_at = mod4(m2[p] + offsets[j])
            left, right = mod4(m3[p] - 1), mod4(m3[p] + 1)
            for copy in subs[p][j]:
                copy.wait_recv()
            onward[p][j] = (
                send(tok.at[2 * c, p, left, line_at], to(p, 3, 1)),
                send(tok.at[2 * c + 1, p, right, line_at], to(p, 3, -1)),
            )
            passed[p][j] = (send(line(p, left, line_at), sib), send(line(p, right, line_at), sib))

    def near_unit(j):
        for p in parts:
            for copy in passed[p][j]:
                copy.wait_recv()
        ffn([(p, mod4(m3[p] + side), mod4(m2[p] + offsets[j])) for p in parts for side in (-1, 1)])

    def settle(j):
        for p in parts:
            for copy in onward[p][j]:
                copy.wait_recv()
            opposite[p][j] = send(line(p, mod4(m3[p] + 2), mod4(m2[p] + offsets[j])), sib)

    def far_unit(lines):
        for p in parts:
            for j in lines:
                opposite[p][j].wait_recv()
        ffn([(p, mod4(m3[p] + 2), mod4(m2[p] + offsets[j])) for p in parts for j in lines])

    own_unit((0, 1))
    for p in parts:
        for copy in ring2b[p]:
            copy.wait_recv()
        region = line(p, m3[p], mod4(m2[p] + 2))
        subs[p][3] = (send(region, to(p, 3, 1)), send(region, to(p, 3, -1)))
        own_line[p][3] = send(region, sib)
    forward(0)
    own_unit((2, 3))
    down_copy = copies.start(down_hbm.at[:, other_half], dsib_out, sib)
    forward(1)
    near_unit(0)
    forward(2)
    near_unit(1)
    forward(3)
    near_unit(2)
    settle(0)
    settle(1)
    near_unit(3)
    settle(2)
    settle(3)
    far_unit((0, 1))
    far_unit((2, 3))

    copies.finish()
    down_copy.wait_recv()
    whole = pltpu.make_async_remote_copy(
        src_ref=hid,
        dst_ref=hid_out.at[1 - c],
        send_sem=hsend_sem,
        recv_sem=hrecv_sem,
        device_id=sib,
        device_id_type=MESH,
    )
    whole.wait_send()
    whole.wait_recv()
    pltpu.make_async_copy(hid, hid_out.at[c], hloc_sem).wait()


def expert_hidden(normed, route, gate_w, up_w, down_w):
    any_space = pl.BlockSpec(memory_space=pl.ANY)
    vmem = pl.BlockSpec(memory_space=pltpu.VMEM)
    count = 1 + SLOTS * (4 + 4 + 16 + 16)
    return pl.pallas_call(
        gather_kernel,
        out_shape=(
            jax.ShapeDtypeStruct((2, SLOTS, 4, 4, 64, 768), BF),
            jax.ShapeDtypeStruct((768, 2048), BF),
        ),
        in_specs=[vmem, vmem, any_space, any_space, any_space],
        out_specs=(any_space, any_space),
        scratch_shapes=[
            pltpu.VMEM((4, SLOTS, 4, 4, 4, 16, 1024), BF),
            pltpu.VMEM((4096, 768), BF),
            pltpu.VMEM((4096, 768), BF),
            pltpu.VMEM((SLOTS, 4, 4, 64, 768), BF),
            pltpu.SemaphoreType.DMA((count,)),
            pltpu.SemaphoreType.DMA((count,)),
            pltpu.SemaphoreType.DMA((2,)),
            pltpu.SemaphoreType.DMA,
            pltpu.SemaphoreType.DMA,
            pltpu.SemaphoreType.DMA,
        ],
        compiler_params=pltpu.CompilerParams(
            collective_id=1, has_side_effects=True, vmem_limit_bytes=60 * 1024 * 1024
        ),
        name="gather_hidden",
    )(normed, route, gate_w, up_w, down_w)


def scatter_kernel(
    hid_hbm, down_hbm, dsib_hbm, res_ref,
    out_ref,
    hv, dw, part_sum, far3, near3, far2, near2, far1, near1, fin,
    send_sem, recv_sem, load_sem,
):
    here = Place()
    c = here.core
    sib = here.sibling()
    parts = range(SLOTS)
    m1 = [here.at(ORDER[p][0]) for p in parts]
    m2 = [here.at(ORDER[p][1]) for p in parts]
    m3 = [here.at(ORDER[p][2]) for p in parts]
    my_half = pl.ds(pl.multiple_of(c * 2048, 2048), 2048)
    loads = {}

    def load(src, dst):
        copy = pltpu.make_async_copy(src, dst, load_sem.at[len(loads)])
        copy.start()
        loads[len(loads)] = copy
        return copy

    loaded_w = [load(down_hbm.at[:, my_half], dw.at[c]), load(dsib_hbm, dw.at[1 - c])]
    planes = (2, 1, -1, 0)
    loaded_h = {}
    for off in planes:
        for p in parts:
            at = mod4(m3[p] + off)
            loaded_h[off, p] = load(hid_hbm.at[:, p, at], hv.at[:, p, at])
    here.greet(("x", "y", "z"))
    copies = Copies(send_sem, recv_sem)

    def to(p, axis_at, step):
        return here.to(ORDER[p][axis_at - 1], step)

    for copy in loaded_w:
        copy.wait()

    def down(p, off):
        at = mod4(m3[p] + off)
        loaded_h[off, p].wait()

        def tile(n, carry):
            cols = pl.ds(pl.multiple_of(n * 1024, 1024), 1024)
            total = jnp.dot(hv[0, p, at].reshape(256, 768), dw[0, :, cols], preferred_element_type=F32)
            total += jnp.dot(hv[1, p, at].reshape(256, 768), dw[1, :, cols], preferred_element_type=F32)
            part_sum[n, p, at] = total.astype(BF).reshape(4, 64, 1024)
            return carry

        lax.fori_loop(0, 2, tile, 0)

    def add(ref, *others):
        total = ref[...].astype(F32)
        for other in others:
            total += other[...].astype(F32)
        ref[...] = total.astype(BF)

    lines = (2, 1, -1, 0)

    def at_line(p, k):
        return mod4(m2[p] + lines[k])

    far_copy, near_copy = {}, {}

    def pass_far(p, k):
        at, l = mod4(m3[p] + 2), at_line(p, k)
        far_copy[p, k] = (
            copies.start(part_sum.at[0, p, at, l], far3.at[0, p, k], to(p, 3, 1)),
            copies.start(part_sum.at[1, p, at, l], far3.at[1, p, k], to(p, 3, -1)),
        )

    def pass_free(p, k):
        l = at_line(p, k)
        right, left = mod4(m3[p] + 1), mod4(m3[p] - 1)
        near_copy[p, k] = [
            copies.start(part_sum.at[1, p, right, l], near3.at[0, 1, p, k], to(p, 3, 1)),
            copies.start(part_sum.at[0, p, left, l], near3.at[1, 0, p, k], to(p, 3, -1)),
        ]

    def pass_bound(p, k):
        l = at_line(p, k)
        right, left = mod4(m3[p] + 1), mod4(m3[p] - 1)
        for copy in far_copy[p, k]:
            copy.wait_recv()
        add(part_sum.at[0, p, right, l], far3.at[0, p, k])
        add(part_sum.at[1, p, left, l], far3.at[1, p, k])
        near_copy[p, k] += [
            copies.start(part_sum.at[0, p, right, l], near3.at[0, 0, p, k], to(p, 3, 1)),
            copies.start(part_sum.at[1, p, left, l], near3.at[1, 1, p, k], to(p, 3, -1)),
        ]

    def take_near(p, k):
        for copy in near_copy[p, k]:
            copy.wait_recv()
        for q in range(2):
            add(part_sum.at[q, p, m3[p], at_line(p, k)], near3.at[0, q, p, k], near3.at[1, q, p, k])

    for p in parts:
        down(p, 2)
        for k in range(4):
            pass_far(p, k)
    for p in parts:
        down(p, 1)
        down(p, -1)
        for k in range(4):
            pass_free(p, k)
    for k in range(2):
        for p in parts:
            pass_bound(p, k)
    for p in parts:
        down(p, 0)
    far2_copy, near2_copy = {}, {}
    for p in parts:
        take_near(p, 0)
        l = at_line(p, 0)
        far2_copy[p] = (
            copies.start(part_sum.at[0, p, m3[p], l], far2.at[0, p], to(p, 2, 1)),
            copies.start(part_sum.at[1, p, m3[p], l], far2.at[1, p], to(p, 2, -1)),
        )
    for k in (2, 3):
        for p in parts:
            pass_bound(p, k)
    for k, side in ((1, 0), (2, 1)):
        for p in parts:
            take_near(p, k)
            l = at_line(p, k)
            far2_copy[p][side].wait_recv()
            add(part_sum.at[side, p, m3[p], l], far2.at[side, p])
            near2_copy[p, side] = copies.start(
                part_sum.at[:, p, m3[p], l], near2.at[side, :, p], to(p, 2, 1 if side == 0 else -1)
            )
    far1_copy, near1_copy = {}, {}

    def block(p, step):
        return pl.ds(pl.multiple_of(mod4(m1[p] + step) * 16, 16), 16)

    for p in parts:
        take_near(p, 3)
    for p in parts:
        for side in range(2):
            near2_copy[p, side].wait_recv()
        for q in range(2):
            add(part_sum.at[q, p, m3[p], m2[p]], near2.at[0, q, p], near2.at[1, q, p])
        far1_copy[p] = (
            copies.start(part_sum.at[0, p, m3[p], m2[p], block(p, 2)], far1.at[0, p], to(p, 1, 1)),
            copies.start(part_sum.at[1, p, m3[p], m2[p], block(p, 2)], far1.at[1, p], to(p, 1, -1)),
        )
    for p in parts:
        for side, step in ((0, 1), (1, -1)):
            far1_copy[p][side].wait_recv()
            add(part_sum.at[side, p, m3[p], m2[p], block(p, step)], far1.at[side, p])
            near1_copy[p, side] = copies.start(
                part_sum.at[:, p, m3[p], m2[p], block(p, step)], near1.at[side, :, p], to(p, 1, step)
            )
    for p in parts:
        for side in range(2):
            near1_copy[p, side].wait_recv()
        for q in range(2):
            total = part_sum[q, p, m3[p], m2[p], block(p, 0)].astype(F32)
            total += near1[0, q, p].astype(F32) + near1[1, q, p].astype(F32)
            total += res_ref[p, :, q * 1024 : q * 1024 + 1024]
            fin[0, p, :, q * 1024 : q * 1024 + 1024] = total[:8]
            fin[1, p, :, q * 1024 : q * 1024 + 1024] = total[8:]
    last = copies.start(fin.at[1 - c], out_ref.at[c], sib)
    out_ref[c] = fin[c]
    last.wait_recv()
    copies.finish()


def expert_sum(hidden, down_w, down_sib, residual):
    any_space = pl.BlockSpec(memory_space=pl.ANY)
    vmem = pl.BlockSpec(memory_space=pltpu.VMEM)
    count = SLOTS * (8 + 16 + 4 + 4) + 1
    return pl.pallas_call(
        scatter_kernel,
        out_shape=jax.ShapeDtypeStruct((2, SLOTS, 8, 2048), F32),
        in_specs=[any_space, any_space, any_space, vmem],
        out_specs=vmem,
        scratch_shapes=[
            pltpu.VMEM((2, SLOTS, 4, 4, 64, 768), BF),
            pltpu.VMEM((2, 768, 2048), BF),
            pltpu.VMEM((2, SLOTS, 4, 4, 64, 1024), BF),
            pltpu.VMEM((2, SLOTS, 4, 64, 1024), BF),
            pltpu.VMEM((2, 2, SLOTS, 4, 64, 1024), BF),
            pltpu.VMEM((2, SLOTS, 64, 1024), BF),
            pltpu.VMEM((2, 2, SLOTS, 64, 1024), BF),
            pltpu.VMEM((2, SLOTS, 16, 1024), BF),
            pltpu.VMEM((2, 2, SLOTS, 16, 1024), BF),
            pltpu.VMEM((2, SLOTS, 8, 2048), F32),
            pltpu.SemaphoreType.DMA((count,)),
            pltpu.SemaphoreType.DMA((count,)),
            pltpu.SemaphoreType.DMA((14,)),
        ],
        compiler_params=pltpu.CompilerParams(
            collective_id=2, has_side_effects=True, vmem_limit_bytes=60 * 1024 * 1024
        ),
        name="down_scatter",
    )(hidden, down_w, down_sib, residual)


def attend(q, k, v):
    scores = lax.dot_general(q, k, (((1,), (1,)), ((), ())), preferred_element_type=F32)
    scores = scores * (1.0 / math.sqrt(DH))
    raised = jnp.exp(scores - jnp.max(scores, axis=-1, keepdims=True))
    weights = (raised / jnp.sum(raised, axis=-1, keepdims=True)).astype(BF)
    return jnp.dot(weights, v, preferred_element_type=F32)


def attention_kernel(
    msg, route_ref, state_ref, gain_ref, proj_hbm,
    norm_out, res_out, route_out,
    got, mixed, ow, sib_state, part_sum, far_a, near_a, far_b, near_b, squares,
    send_sem, recv_sem, load_sem,
):
    here = Place()
    c = here.core
    sib = here.sibling()
    chip = here.z * 4 + here.x

    my_half = pl.ds(pl.multiple_of(c * 2048, 2048), 2048)
    other_half = pl.ds(pl.multiple_of((1 - c) * 2048, 2048), 2048)
    my_rows = pl.ds(pl.multiple_of(c * DH, DH), DH)
    load = pltpu.make_async_copy(proj_hbm.at[:, my_half], ow.at[my_rows], load_sem)
    load.start()

    hops = [(dz, dx) for dz in range(4) for dx in range(4) if (dz, dx) != (0, 0)]
    hops.sort(key=lambda hop: -(min(hop[0], 4 - hop[0]) + min(hop[1], 4 - hop[1])))

    def chip_at(dz, dx):
        return lax.rem(here.z + dz, 4) * 4 + lax.rem(here.x + dx, 4)

    barrier = pltpu.get_barrier_semaphore()
    others = [(here.y, chip_at(dz, dx) * 2 + c) for dz, dx in hops]
    greeted = others + [here.to("y", 1), here.to("y", -1), sib]
    for other in greeted:
        pl.semaphore_signal(barrier, inc=1, device_id=other, device_id_type=MESH)
    pl.semaphore_wait(barrier, len(greeted))

    copies = Copies(send_sem, recv_sem)
    arriving = []
    for (dz, dx), other in zip(hops, others):
        arriving.append(copies.start(msg.at[chip_at(dz, dx)], got.at[c, chip], other))
    got[c, chip] = msg[chip]
    route_out[here.y, here.z, here.x, c] = route_ref[...]
    tile = route_out.at[here.y, here.z, here.x, c]
    route_swap = copies.start(tile, tile, sib)
    proj_copy = copies.start(proj_hbm.at[:, other_half], ow.at[my_rows], sib)
    state_copy = copies.start(state_ref.at[1 - c], sib_state, sib)

    def ring(region, axis):
        return (copies.start(region, region, here.to(axis, 1)), copies.start(region, region, here.to(axis, -1)))

    route_swap.wait_recv()
    along_x = ring(route_out.at[here.y, here.z, here.x], "x")
    for copy in arriving:
        copy.wait_recv()
    passed = copies.start(got.at[c], got.at[c], sib)
    for copy in along_x:
        copy.wait_recv()
    left = route_out.at[here.y, here.z, mod4(here.x - 1)]
    far_x = copies.start(left, left, here.to("x", 1))
    passed.wait_recv()
    for s in range(SLOTS):
        held = got[:, :, s].astype(F32)
        q = jnp.where(c == 0, held[:, :, 0, :8], held[:, :, 0, 8:]).reshape(256, DH).astype(BF)
        k = held[:, :, 1, :8].reshape(256, DH).astype(BF)
        v = held[:, :, 1, 8:].reshape(256, DH).astype(BF)
        out = attend(q, k, v).reshape(2, 4, 4, 8, DH)
        mixed[c, :, :, s] = jnp.concatenate([out[0], out[1]], axis=2).astype(BF)
    mixed_copy = copies.start(mixed.at[c], mixed.at[c], sib)
    far_x.wait_recv()
    along_z = ring(route_out.at[here.y, here.z], "z")
    load.wait()
    proj_copy.wait_recv()
    mixed_copy.wait_recv()

    axes = (("z", "x"), ("x", "z"))
    m2 = [here.at(axes[t][0]) for t in range(2)]
    m1 = [here.at(axes[t][1]) for t in range(2)]

    def project(t, off):
        at = mod4(m2[t] + off)
        rows = [(mixed[h, at] if t == 0 else mixed[h, :, at]).reshape(192, DH) for h in range(2)]
        rows = jnp.concatenate(rows, axis=1)
        for half in range(2):
            first = t * 1024 + half * 512
            total = jnp.dot(rows, ow[:, first : first + 512], preferred_element_type=F32)
            part_sum[half, t, at] = total.astype(BF).reshape(4, 48, 512)

    def add(ref, *terms):
        total = ref[...].astype(F32)
        for term in terms:
            total += term[...].astype(F32)
        ref[...] = total.astype(BF)

    lines = (2, 1, -1, 0)
    far_copy, near_copy = {}, {}
    for t in range(2):
        project(t, 2)
        at = mod4(m2[t] + 2)
        for k in range(4):
            l = mod4(m1[t] + lines[k])
            far_copy[t, k] = (
                copies.start(part_sum.at[0, t, at, l], far_a.at[0, t, k], here.to(axes[t][0], 1)),
                copies.start(part_sum.at[1, t, at, l], far_a.at[1, t, k], here.to(axes[t][0], -1)),
            )
    for t in range(2):
        project(t, 1)
        project(t, -1)
    for k in range(4):
        for t in range(2):
            l = mod4(m1[t] + lines[k])
            right, left = mod4(m2[t] + 1), mod4(m2[t] - 1)
            to_right, to_left = here.to(axes[t][0], 1), here.to(axes[t][0], -1)
            near_copy[t, k] = [
                copies.start(part_sum.at[1, t, right, l], near_a.at[0, 1, t, k], to_right),
                copies.start(part_sum.at[0, t, left, l], near_a.at[1, 0, t, k], to_left),
            ]
            for copy in far_copy[t, k]:
                copy.wait_recv()
            add(part_sum.at[0, t, right, l], far_a.at[0, t, k])
            add(part_sum.at[1, t, left, l], far_a.at[1, t, k])
            near_copy[t, k] += [
                copies.start(part_sum.at[0, t, right, l], near_a.at[0, 0, t, k], to_right),
                copies.start(part_sum.at[1, t, left, l], near_a.at[1, 1, t, k], to_left),
            ]
        if k == 0:
            for t in range(2):
                project(t, 0)
            for copy in along_z:
                copy.wait_recv()
            behind = route_out.at[here.y, mod4(here.z - 1)]
            far_z = copies.start(behind, behind, here.to("z", 1))

    far_z.wait_recv()
    along_y = ring(route_out.at[here.y], "y")

    def take_near(t, k):
        for copy in near_copy[t, k]:
            copy.wait_recv()
        l = mod4(m1[t] + lines[k])
        for half in range(2):
            add(part_sum.at[half, t, m2[t], l], near_a.at[0, half, t, k], near_a.at[1, half, t, k])

    far_b_copy, near_b_copy = {}, {}
    for t in range(2):
        take_near(t, 0)
        l = mod4(m1[t] + 2)
        far_b_copy[t] = (
            copies.start(part_sum.at[0, t, m2[t], l], far_b.at[0, t], here.to(axes[t][1], 1)),
            copies.start(part_sum.at[1, t, m2[t], l], far_b.at[1, t], here.to(axes[t][1], -1)),
        )
    for k, side, step in ((1, 0, 1), (2, 1, -1)):
        for t in range(2):
            take_near(t, k)
            l = mod4(m1[t] + step)
            far_b_copy[t][side].wait_recv()
            add(part_sum.at[side, t, m2[t], l], far_b.at[side, t])
            near_b_copy[t, side] = copies.start(
                part_sum.at[:, t, m2[t], l], near_b.at[side, :, t], here.to(axes[t][1], step)
            )
    for copy in along_y:
        copy.wait_recv()
    behind = route_out.at[mod4(here.y - 1)]
    far_y = copies.start(behind, behind, here.to("y", 1))
    state_copy.wait_recv()
    square = jnp.zeros((48, 1), F32)
    for t in range(2):
        for copy in near_copy[t, 3]:
            copy.wait_recv()
        for side in range(2):
            near_b_copy[t, side].wait_recv()
        for half in range(2):
            total = part_sum[half, t, m2[t], m1[t]].astype(F32)
            for side in range(2):
                total += near_a[side, half, t, 3].astype(F32)
            for side in range(2):
                total += near_b[side, half, t].astype(F32)
            first = t * 1024 + half * 512
            cols = slice(first, first + 512)
            mine = state_ref[c, :, :, cols]
            theirs = sib_state[:, :, cols]
            low = jnp.where(c == 0, mine, theirs)
            high = jnp.where(c == 0, theirs, mine)
            total += jnp.concatenate([low, high], axis=1).reshape(48, 512)
            res_out[:, :, cols] = total.reshape(SLOTS, 16, 512)
            square += jnp.sum(total * total, axis=1, keepdims=True)
    squares[c] = jnp.broadcast_to(square, (48, 128))
    square_copy = copies.start(squares.at[c], squares.at[c], sib)
    square_copy.wait_recv()
    mean = (squares[0, :, :1] + squares[1, :, :1]) * (1.0 / 4096.0)
    factor = lax.rsqrt(mean + 1e-06).reshape(SLOTS, 16, 1)
    for h in range(2):
        cols = slice(h * 1024, h * 1024 + 1024)
        gain = gain_ref[pl.ds(c, 1), cols].reshape(1, 1, 1024)
        norm_out[h] = (res_out[:, :, cols] * factor * gain).astype(BF)
    far_y.wait_recv()
    copies.finish()


def attention(msg, route, state, gain, out_proj):
    any_space = pl.BlockSpec(memory_space=pl.ANY)
    vmem = pl.BlockSpec(memory_space=pltpu.VMEM)
    count = 15 + 1 + 1 + 1 + 1 + 1 + 2 * (8 + 16 + 2 + 2) + 9 + 1
    return pl.pallas_call(
        attention_kernel,
        out_shape=(
            jax.ShapeDtypeStruct((2, SLOTS, 16, 1024), BF),
            jax.ShapeDtypeStruct((SLOTS, 16, 2048), F32),
            jax.ShapeDtypeStruct((4, 4, 4, 2, 8, 128), F32),
        ),
        in_specs=[vmem, vmem, vmem, vmem, any_space],
        out_specs=(vmem, vmem, vmem),
        scratch_shapes=[
            pltpu.VMEM((2, 16, SLOTS, 2, 16, DH), BF),
            pltpu.VMEM((2, 4, 4, SLOTS, 16, DH), BF),
            pltpu.VMEM((2 * DH, 2048), BF),
            pltpu.VMEM((SLOTS, 8, 2048), F32),
            pltpu.VMEM((2, 2, 4, 4, 48, 512), BF),
            pltpu.VMEM((2, 2, 4, 48, 512), BF),
            pltpu.VMEM((2, 2, 2, 4, 48, 512), BF),
            pltpu.VMEM((2, 2, 48, 512), BF),
            pltpu.VMEM((2, 2, 2, 48, 512), BF),
            pltpu.VMEM((2, 48, 128), F32),
            pltpu.SemaphoreType.DMA((count,)),
            pltpu.SemaphoreType.DMA((count,)),
            pltpu.SemaphoreType.DMA,
        ],
        compiler_params=pltpu.CompilerParams(
            collective_id=3, has_side_effects=True, vmem_limit_bytes=48 * 1024 * 1024
        ),
        name="attention_norm",
    )(msg, route, state, gain, out_proj)


def on_device(
    states, query_in, key_in, value_in, cached_delta, recompute, expert_ids, expert_weights,
    norm_gain, out_proj, gate_proj, up_proj, down_proj,
):
    dev_count = lax.axis_size("dev")
    req_here, seq_here, features = states.shape
    rank = jnp.cumsum(recompute) - 1
    live_count = jnp.sum(recompute)
    idle_rank = live_count + jnp.cumsum(1 - recompute) - 1
    place = jnp.where(recompute == 1, rank, idle_rank)
    pick = (place[None, :] == jnp.arange(SLOTS, dtype=jnp.int32)[:, None]).astype(jnp.int32)
    chosen = jnp.sum(pick * jnp.arange(req_here, dtype=jnp.int32)[None, :], axis=1)
    live_slot = jnp.arange(SLOTS, dtype=jnp.int32) < live_count

    def select(whole):
        return jnp.concatenate(
            [lax.dynamic_slice_in_dim(whole, chosen[s], 1, 0) for s in range(SLOTS)], axis=0
        )

    ids = select(expert_ids.reshape(req_here, seq_here, -1))
    weights = select(expert_weights.reshape(req_here, seq_here, -1))
    experts = jnp.arange(dev_count, dtype=jnp.int32)
    dense = jnp.sum(
        jnp.where(ids[..., None] == experts, weights[..., None], 0.0), axis=2
    )
    dense = jnp.where(live_slot[:, None, None], dense, 0.0)
    route = dense.transpose(1, 0, 2).reshape(seq_here, -1)
    route = jnp.pad(route, ((0, 0), (0, 128 - SLOTS * dev_count)))

    chips = dev_count // 2
    queries = select(query_in).reshape(SLOTS, seq_here, chips, 2, DH).transpose(2, 0, 3, 1, 4)
    keys = select(key_in).reshape(SLOTS, seq_here, KV_HEADS, DH)
    values = select(value_in).reshape(SLOTS, seq_here, KV_HEADS, DH)
    both = jnp.stack([keys, values]).transpose(3, 1, 0, 2, 4)
    both = jnp.repeat(both, chips // KV_HEADS, axis=0)
    msg = jnp.stack(
        [queries.reshape(chips, SLOTS, 16, DH), both.reshape(chips, SLOTS, 16, DH)], axis=2
    )
    state = select(states).astype(F32).reshape(SLOTS, seq_here, 2, 2048).transpose(2, 0, 1, 3)
    normed, residual, routes = attention(msg, route, state, norm_gain.reshape(2, 2048), out_proj)
    hidden, down_sib = expert_hidden(normed, routes, gate_proj[0], up_proj[0], down_proj[0])
    fresh = expert_sum(hidden, down_proj[0], down_sib, residual)
    fresh = fresh.transpose(1, 2, 0, 3).reshape(SLOTS, seq_here, features)
    reused = states.astype(jnp.float32) + cached_delta.astype(jnp.float32)
    spread = sum(
        jnp.where((place == s)[:, None, None], fresh[s][None], 0.0) for s in range(SLOTS)
    )
    layer_out = jnp.where((recompute == 1)[:, None, None], spread, reused)
    return layer_out.astype(jnp.bfloat16)


def solution(mesh):
    return jax.shard_map(
        on_device,
        mesh=mesh,
        in_specs=(
            P("grp", "dev", None),
            P("grp", "dev", None),
            P("grp", "dev", None),
            P("grp", "dev", None),
            P("grp", "dev", None),
            P("grp"),
            P(("grp", "dev"), None),
            P(("grp", "dev"), None),
            P(),
            P("dev", None),
            P("dev", None, "grp"),
            P("dev", None, "grp"),
            P("dev", "grp", None),
        ),
        out_specs=P("grp", "dev", None),
        check_vma=False,
    )
```

```python
import math

import jax
import jax.numpy as jnp
from jax import lax
from jax.experimental import pallas as pl
from jax.experimental.pallas import tpu as pltpu
from jax.sharding import PartitionSpec as P

HEADS = 32
KV_HEADS = 8
DH = 128
SLOTS = 3
BF = jnp.bfloat16
F32 = jnp.float32
MESH = pl.DeviceIdType.MESH
ORDER = (("x", "z", "y"), ("z", "y", "x"), ("y", "x", "z"))


def mod4(v):
    return lax.rem(v + 4, 4)


class Place:
    def __init__(self):
        self.y = lax.axis_index("grp")
        dev = lax.axis_index("dev")
        self.core = lax.rem(dev, 2)
        self.x = lax.rem(lax.div(dev, 2), 4)
        self.z = lax.div(dev, 8)

    def at(self, axis):
        return {"x": self.x, "y": self.y, "z": self.z}[axis]

    def to(self, axis, step):
        y, x, z = self.y, self.x, self.z
        if axis == "y":
            y = mod4(y + step)
        elif axis == "x":
            x = mod4(x + step)
        else:
            z = mod4(z + step)
        return (y, (z * 4 + x) * 2 + self.core)

    def sibling(self):
        return (self.y, (self.z * 4 + self.x) * 2 + 1 - self.core)

    def greet(self, axes):
        barrier = pltpu.get_barrier_semaphore()
        others = [self.to(axis, step) for axis in axes for step in (1, -1)]
        others.append(self.sibling())
        for other in others:
            pl.semaphore_signal(barrier, inc=1, device_id=other, device_id_type=MESH)
        pl.semaphore_wait(barrier, len(others))


class Copies:
    def __init__(self, send_sem, recv_sem):
        self.send_sem, self.recv_sem = send_sem, recv_sem
        self.made, self.count = [], 0

    def start(self, src, dst, device):
        k = self.count
        self.count += 1
        copy = pltpu.make_async_remote_copy(
            src_ref=src,
            dst_ref=dst,
            send_sem=self.send_sem.at[k],
            recv_sem=self.recv_sem.at[k],
            device_id=device,
            device_id_type=MESH,
        )
        copy.start()
        self.made.append(copy)
        return copy

    def finish(self):
        for copy in self.made:
            copy.wait_send()


def experts_kernel(
    norm_ref, route_ref, res_ref, gate_hbm, up_hbm, down_hbm,
    out_ref,
    tok, wg, wu, hv, dw, free3, fin, send_sem, recv_sem, load_sem, ready,
):
    here = Place()
    c = here.core
    sib = here.sibling()
    my_half = pl.ds(pl.multiple_of(c * 2048, 2048), 2048)
    load_g = pltpu.make_async_copy(gate_hbm, wg, load_sem.at[0])
    load_u = pltpu.make_async_copy(up_hbm, wu, load_sem.at[1])
    load_d = pltpu.make_async_copy(down_hbm.at[:, my_half], dw.at[c], load_sem.at[2])
    load_g.start()
    load_u.start()
    load_d.start()
    here.greet(("x", "y", "z"))
    copies = Copies(send_sem, recv_sem)
    m1 = [here.at(ORDER[p][0]) for p in range(SLOTS)]
    m2 = [here.at(ORDER[p][1]) for p in range(SLOTS)]
    m3 = [here.at(ORDER[p][2]) for p in range(SLOTS)]
    parts = range(SLOTS)

    def to(p, axis_at, step):
        return here.to(ORDER[p][axis_at - 1], step)

    other_half = pl.ds(pl.multiple_of((1 - c) * 2048, 2048), 2048)
    pair = pl.ds(2 * c, 2)
    for p in parts:
        for h in range(2):
            tok[2 * c + h, p, m3[p], m2[p], m1[p]] = norm_ref[h, p]

    moved = []

    def send(region, device):
        moved.append(copies.start(region, region, device))
        return moved[-1]

    first = []
    for p in parts:
        block = tok.at[pair, p, m3[p], m2[p], m1[p]]
        first.append((send(block, to(p, 1, 1)), send(block, to(p, 1, -1))))
    second = []
    for p in parts:
        for copy in first[p]:
            copy.wait_recv()
        second.append((
            send(tok.at[2 * c, p, m3[p], m2[p], mod4(m1[p] - 1)], to(p, 1, 1)),
            send(tok.at[2 * c + 1, p, m3[p], m2[p], mod4(m1[p] + 1)], to(p, 1, -1)),
        ))

    def line(p, c3, c2):
        return tok.at[pair, p, c3, c2]

    own_line = [{} for p in parts]
    ring2 = []
    subs = [[None] * 4 for p in parts]
    offsets = (0, 1, -1, 2)
    for p in parts:
        for copy in second[p]:
            copy.wait_recv()
        region = line(p, m3[p], m2[p])
        ring2.append((send(region, to(p, 2, 1)), send(region, to(p, 2, -1))))
        own_line[p][0] = send(region, sib)
    for p in parts:
        region = line(p, m3[p], m2[p])
        subs[p][0] = (send(region, to(p, 3, 1)), send(region, to(p, 3, -1)))
    ring2b = []
    for p in parts:
        for copy in ring2[p]:
            copy.wait_recv()
        ring2b.append((
            send(tok.at[2 * c, p, m3[p], mod4(m2[p] - 1)], to(p, 2, 1)),
            send(tok.at[2 * c + 1, p, m3[p], mod4(m2[p] + 1)], to(p, 2, -1)),
        ))
        for j in (1, 2):
            own_line[p][j] = send(line(p, m3[p], mod4(m2[p] + offsets[j])), sib)
    for j in (1, 2):
        for p in parts:
            region = line(p, m3[p], mod4(m2[p] + offsets[j]))
            subs[p][j] = (send(region, to(p, 3, 1)), send(region, to(p, 3, -1)))

    load_g.wait()
    load_u.wait()

    handed = [[] for p in parts]
    expert = lax.axis_index("dev")
    lane = lax.broadcasted_iota(jnp.int32, (64, 128), 1)

    def weight_of(p, c3, c2):
        index = ((c3, c2), (c2, slice(None), c3), (slice(None), c3, c2))[p]
        held = route_ref[index].reshape(64, 128)
        return jnp.sum(jnp.where(lane == p * 32 + expert, held, 0.0), axis=1, keepdims=True)

    def ffn(pieces):
        weights = [weight_of(*piece) for piece in pieces]

        def tile(n, carry):
            cols = pl.ds(pl.multiple_of(n * 256, 256), 256)
            gate = jnp.zeros((64 * len(pieces), 256), F32)
            up = jnp.zeros((64 * len(pieces), 256), F32)
            for q in range(4):
                rows = jnp.concatenate([tok[q, p, c3, c2].reshape(64, 1024) for p, c3, c2 in pieces], axis=0)
                depth = pl.ds(q * 1024, 1024)
                gate += jnp.dot(rows, wg[depth, cols], preferred_element_type=F32)
                up += jnp.dot(rows, wu[depth, cols], preferred_element_type=F32)
            act = gate / (1.0 + jnp.exp(-gate)) * up
            for i, (p, c3, c2) in enumerate(pieces):
                hv[c, p, c3, c2, :, cols] = (act[64 * i : 64 * i + 64] * weights[i]).astype(BF)
            return carry

        lax.fori_loop(0, 3, tile, 0)
        for p, c3, c2 in pieces:
            piece = hv.at[c, p, c3, c2]
            handed[p].append(copies.start(piece, piece, sib))

    def own_unit(lines):
        for p in parts:
            for j in lines:
                own_line[p][j].wait_recv()
        ffn([(p, m3[p], mod4(m2[p] + offsets[j])) for p in parts for j in lines])

    passed = [[None] * 4 for p in parts]
    onward = [[None] * 4 for p in parts]
    opposite = [[None] * 4 for p in parts]

    def forward(j):
        for p in parts:
            line_at = mod4(m2[p] + offsets[j])
            left, right = mod4(m3[p] - 1), mod4(m3[p] + 1)
            for copy in subs[p][j]:
                copy.wait_recv()
            onward[p][j] = (
                send(tok.at[2 * c, p, left, line_at], to(p, 3, 1)),
                send(tok.at[2 * c + 1, p, right, line_at], to(p, 3, -1)),
            )
            passed[p][j] = (send(line(p, left, line_at), sib), send(line(p, right, line_at), sib))

    def near_unit(j):
        for p in parts:
            for copy in passed[p][j]:
                copy.wait_recv()
        ffn([(p, mod4(m3[p] + side), mod4(m2[p] + offsets[j])) for p in parts for side in (-1, 1)])

    def settle(j):
        for p in parts:
            for copy in onward[p][j]:
                copy.wait_recv()
            opposite[p][j] = send(line(p, mod4(m3[p] + 2), mod4(m2[p] + offsets[j])), sib)

    def far_unit(lines):
        for p in parts:
            for j in lines:
                opposite[p][j].wait_recv()
        ffn([(p, mod4(m3[p] + 2), mod4(m2[p] + offsets[j])) for p in parts for j in lines])

    def part(n, p, c3, c2):
        return tok.at[2 * (1 - c) + n, p, c3, c2]

    both = pl.ds(2 * (1 - c), 2)

    def down(p, off, n):
        at = mod4(m3[p] + off)
        total = jnp.dot(hv[0, p, at].reshape(256, 768), dw[0, :, n * 1024 : n * 1024 + 1024], preferred_element_type=F32)
        total += jnp.dot(hv[1, p, at].reshape(256, 768), dw[1, :, n * 1024 : n * 1024 + 1024], preferred_element_type=F32)
        tok[2 * (1 - c) + n, p, at] = total.astype(BF).reshape(4, 4, 16, 1024)

    def add(ref, *others):
        total = ref[...].astype(F32)
        for other in others:
            total += other[...].astype(F32)
        ref[...] = total.astype(BF)

    lines = (2, 1, -1, 0)

    def at_line(p, k):
        return mod4(m2[p] + lines[k])

    def take_handed():
        for p in parts:
            for copy in handed[p]:
                copy.wait_recv()
            handed[p].clear()

    far_copy, near_copy = {}, {}

    def pass_free(p, k):
        l = at_line(p, k)
        right, left = mod4(m3[p] + 1), mod4(m3[p] - 1)
        near_copy[p, k] = [
            copies.start(part(1, p, right, l), free3.at[0, p, k], to(p, 3, 1)),
            copies.start(part(0, p, left, l), free3.at[1, p, k], to(p, 3, -1)),
        ]

    def pass_far(p, k):
        at, l = mod4(m3[p] + 2), at_line(p, k)
        far_copy[p, k] = (
            copies.start(part(0, p, at, l), tok.at[2 * c, p, 0, k], to(p, 3, 1)),
            copies.start(part(1, p, at, l), tok.at[2 * c + 1, p, 0, k], to(p, 3, -1)),
        )

    def pass_bound(p, k):
        l = at_line(p, k)
        right, left = mod4(m3[p] + 1), mod4(m3[p] - 1)
        for copy in far_copy[p, k]:
            copy.wait_recv()
        add(part(0, p, right, l), tok.at[2 * c, p, 0, k])
        add(part(1, p, left, l), tok.at[2 * c + 1, p, 0, k])
        near_copy[p, k] += [
            copies.start(part(0, p, right, l), tok.at[2 * c, p, 1, k], to(p, 3, 1)),
            copies.start(part(1, p, left, l), tok.at[2 * c + 1, p, 1, k], to(p, 3, -1)),
        ]

    def take_near(p, k):
        for copy in near_copy[p, k]:
            copy.wait_recv()
        l = at_line(p, k)
        add(part(0, p, m3[p], l), tok.at[2 * c, p, 1, k], free3.at[1, p, k])
        add(part(1, p, m3[p], l), tok.at[2 * c + 1, p, 1, k], free3.at[0, p, k])

    own_unit((0, 1))
    for p in parts:
        for copy in ring2b[p]:
            copy.wait_recv()
        region = line(p, m3[p], mod4(m2[p] + 2))
        subs[p][3] = (send(region, to(p, 3, 1)), send(region, to(p, 3, -1)))
        own_line[p][3] = send(region, sib)
    forward(0)
    own_unit((2, 3))
    down_copy = copies.start(down_hbm.at[:, other_half], dw.at[c], sib)
    forward(1)
    near_unit(0)
    forward(2)
    near_unit(1)
    forward(3)
    near_unit(2)
    settle(0)
    settle(1)
    near_unit(3)
    settle(2)
    settle(3)
    load_d.wait()
    down_copy.wait_recv()
    take_handed()
    for p in parts:
        down(p, 1, 1)
        down(p, -1, 0)
        for k in range(4):
            pass_free(p, k)
    far_unit((0, 1))
    far_unit((2, 3))
    for copy in moved:
        copy.wait_send()
    done = [id(copy) for copy in moved]
    copies.made = [copy for copy in copies.made if id(copy) not in done]
    neighbours = [here.to(axis, step) for axis in ("x", "y", "z") for step in (1, -1)]
    for other in neighbours:
        pl.semaphore_signal(ready, inc=1, device_id=other, device_id_type=MESH)
    take_handed()
    for p in parts:
        down(p, 2, 0)
        down(p, 2, 1)
        if p == 0:
            pl.semaphore_wait(ready, len(neighbours))
        for k in range(4):
            pass_far(p, k)
    for p in parts:
        down(p, 1, 0)
        down(p, -1, 1)
    for k in range(2):
        for p in parts:
            pass_bound(p, k)
    for p in parts:
        down(p, 0, 0)
        down(p, 0, 1)
    far2_copy, near2_copy = {}, {}
    for p in parts:
        take_near(p, 0)
        l = at_line(p, 0)
        far2_copy[p] = (
            copies.start(part(0, p, m3[p], l), tok.at[2 * c, p, 2, 0], to(p, 2, 1)),
            copies.start(part(1, p, m3[p], l), tok.at[2 * c + 1, p, 2, 0], to(p, 2, -1)),
        )
    for k in (2, 3):
        for p in parts:
            pass_bound(p, k)
    for k, side in ((1, 0), (2, 1)):
        for p in parts:
            take_near(p, k)
            l = at_line(p, k)
            far2_copy[p][side].wait_recv()
            add(part(side, p, m3[p], l), tok.at[2 * c + side, p, 2, 0])
            near2_copy[p, side] = copies.start(
                tok.at[both, p, m3[p], l], tok.at[2 * c + side, p, 2, pl.ds(1, 2)], to(p, 2, 1 if side == 0 else -1)
            )
    far1_copy, near1_copy = {}, {}
    for p in parts:
        take_near(p, 3)
    for p in parts:
        for side in range(2):
            near2_copy[p, side].wait_recv()
        for q in range(2):
            add(part(q, p, m3[p], m2[p]), tok.at[2 * c, p, 2, 1 + q], tok.at[2 * c + 1, p, 2, 1 + q])
        far = mod4(m1[p] + 2)
        far1_copy[p] = (
            copies.start(part(0, p, m3[p], m2[p]).at[far], tok.at[2 * c, p, 3, 0, 0], to(p, 1, 1)),
            copies.start(part(1, p, m3[p], m2[p]).at[far], tok.at[2 * c + 1, p, 3, 0, 0], to(p, 1, -1)),
        )
    for p in parts:
        for side, step in ((0, 1), (1, -1)):
            near = mod4(m1[p] + step)
            far1_copy[p][side].wait_recv()
            add(part(side, p, m3[p], m2[p]).at[near], tok.at[2 * c + side, p, 3, 0, 0])
            near1_copy[p, side] = copies.start(
                tok.at[both, p, m3[p], m2[p], near], tok.at[2 * c + side, p, 3, 1, pl.ds(0, 2)], to(p, 1, step)
            )
    for p in parts:
        for side in range(2):
            near1_copy[p, side].wait_recv()
        for q in range(2):
            total = tok[2 * (1 - c) + q, p, m3[p], m2[p], m1[p]].astype(F32)
            for side in range(2):
                total += tok[2 * c + side, p, 3, 1, q].astype(F32)
            total += res_ref[p, :, q * 1024 : q * 1024 + 1024]
            fin[0, p, :, q * 1024 : q * 1024 + 1024] = total[:8]
            fin[1, p, :, q * 1024 : q * 1024 + 1024] = total[8:]
    last = copies.start(fin.at[1 - c], out_ref.at[c], sib)
    out_ref[c] = fin[c]
    last.wait_recv()
    copies.finish()


def expert_layer(normed, route, residual, gate_w, up_w, down_w):
    any_space = pl.BlockSpec(memory_space=pl.ANY)
    vmem = pl.BlockSpec(memory_space=pltpu.VMEM)
    count = SLOTS * (4 + 4 + 16 + 16 + 16) + 1 + SLOTS * (8 + 16 + 4 + 4) + 1
    return pl.pallas_call(
        experts_kernel,
        out_shape=jax.ShapeDtypeStruct((2, SLOTS, 8, 2048), F32),
        in_specs=[vmem, vmem, vmem, any_space, any_space, any_space],
        out_specs=vmem,
        scratch_shapes=[
            pltpu.VMEM((4, SLOTS, 4, 4, 4, 16, 1024), BF),
            pltpu.VMEM((4096, 768), BF),
            pltpu.VMEM((4096, 768), BF),
            pltpu.VMEM((2, SLOTS, 4, 4, 64, 768), BF),
            pltpu.VMEM((2, 768, 2048), BF),
            pltpu.VMEM((2, SLOTS, 4, 4, 16, 1024), BF),
            pltpu.VMEM((2, SLOTS, 8, 2048), F32),
            pltpu.SemaphoreType.DMA((count,)),
            pltpu.SemaphoreType.DMA((count,)),
            pltpu.SemaphoreType.DMA((3,)),
            pltpu.SemaphoreType.REGULAR,
        ],
        compiler_params=pltpu.CompilerParams(
            collective_id=1, has_side_effects=True, vmem_limit_bytes=62 * 1024 * 1024
        ),
        name="experts_kernel",
    )(normed, route, residual, gate_w, up_w, down_w)


def attend(q, k, v):
    scores = lax.dot_general(q, k, (((1,), (1,)), ((), ())), preferred_element_type=F32)
    scores = scores * (1.0 / math.sqrt(DH))
    raised = jnp.exp(scores - jnp.max(scores, axis=-1, keepdims=True))
    weights = (raised / jnp.sum(raised, axis=-1, keepdims=True)).astype(BF)
    return jnp.dot(weights, v, preferred_element_type=F32)


def attention_kernel(
    msg, route_ref, state_ref, gain_ref, proj_hbm,
    norm_out, res_out, route_out,
    got, mixed, ow, sib_state, part_sum, far_a, near_a, far_b, near_b, squares,
    send_sem, recv_sem, load_sem,
):
    here = Place()
    c = here.core
    sib = here.sibling()
    chip = here.z * 4 + here.x

    my_half = pl.ds(pl.multiple_of(c * 2048, 2048), 2048)
    other_half = pl.ds(pl.multiple_of((1 - c) * 2048, 2048), 2048)
    my_rows = pl.ds(pl.multiple_of(c * DH, DH), DH)
    load = pltpu.make_async_copy(proj_hbm.at[:, my_half], ow.at[my_rows], load_sem)
    load.start()

    hops = [(dz, dx) for dz in range(4) for dx in range(4) if (dz, dx) != (0, 0)]
    hops.sort(key=lambda hop: -(min(hop[0], 4 - hop[0]) + min(hop[1], 4 - hop[1])))

    def chip_at(dz, dx):
        return lax.rem(here.z + dz, 4) * 4 + lax.rem(here.x + dx, 4)

    barrier = pltpu.get_barrier_semaphore()
    others = [(here.y, chip_at(dz, dx) * 2 + c) for dz, dx in hops]
    greeted = others + [here.to("y", 1), here.to("y", -1), sib]
    for other in greeted:
        pl.semaphore_signal(barrier, inc=1, device_id=other, device_id_type=MESH)
    pl.semaphore_wait(barrier, len(greeted))

    copies = Copies(send_sem, recv_sem)
    arriving = []
    for (dz, dx), other in zip(hops, others):
        arriving.append(copies.start(msg.at[chip_at(dz, dx)], got.at[c, chip], other))
    got[c, chip] = msg[chip]
    route_out[here.y, here.z, here.x, c] = route_ref[...]
    tile = route_out.at[here.y, here.z, here.x, c]
    route_swap = copies.start(tile, tile, sib)
    proj_copy = copies.start(proj_hbm.at[:, other_half], ow.at[my_rows], sib)
    state_copy = copies.start(state_ref.at[1 - c], sib_state, sib)

    def ring(region, axis):
        return (copies.start(region, region, here.to(axis, 1)), copies.start(region, region, here.to(axis, -1)))

    route_swap.wait_recv()
    along_x = ring(route_out.at[here.y, here.z, here.x], "x")
    for copy in arriving:
        copy.wait_recv()
    passed = copies.start(got.at[c], got.at[c], sib)
    for copy in along_x:
        copy.wait_recv()
    left = route_out.at[here.y, here.z, mod4(here.x - 1)]
    far_x = copies.start(left, left, here.to("x", 1))
    passed.wait_recv()
    for s in range(SLOTS):
        held = got[:, :, s].astype(F32)
        q = jnp.where(c == 0, held[:, :, 0, :8], held[:, :, 0, 8:]).reshape(256, DH).astype(BF)
        k = held[:, :, 1, :8].reshape(256, DH).astype(BF)
        v = held[:, :, 1, 8:].reshape(256, DH).astype(BF)
        out = attend(q, k, v).reshape(2, 4, 4, 8, DH)
        mixed[c, :, :, s] = jnp.concatenate([out[0], out[1]], axis=2).astype(BF)
    mixed_copy = copies.start(mixed.at[c], mixed.at[c], sib)
    far_x.wait_recv()
    along_z = ring(route_out.at[here.y, here.z], "z")
    load.wait()
    proj_copy.wait_recv()
    mixed_copy.wait_recv()

    axes = (("z", "x"), ("x", "z"))
    m2 = [here.at(axes[t][0]) for t in range(2)]
    m1 = [here.at(axes[t][1]) for t in range(2)]

    def project(t, off):
        at = mod4(m2[t] + off)
        rows = [(mixed[h, at] if t == 0 else mixed[h, :, at]).reshape(192, DH) for h in range(2)]
        rows = jnp.concatenate(rows, axis=1)
        for half in range(2):
            first = t * 1024 + half * 512
            total = jnp.dot(rows, ow[:, first : first + 512], preferred_element_type=F32)
            part_sum[half, t, at] = total.astype(BF).reshape(4, 48, 512)

    def add(ref, *terms):
        total = ref[...].astype(F32)
        for term in terms:
            total += term[...].astype(F32)
        ref[...] = total.astype(BF)

    lines = (2, 1, -1, 0)
    far_copy, near_copy = {}, {}
    for t in range(2):
        project(t, 2)
        at = mod4(m2[t] + 2)
        for k in range(4):
            l = mod4(m1[t] + lines[k])
            far_copy[t, k] = (
                copies.start(part_sum.at[0, t, at, l], far_a.at[0, t, k], here.to(axes[t][0], 1)),
                copies.start(part_sum.at[1, t, at, l], far_a.at[1, t, k], here.to(axes[t][0], -1)),
            )
    for t in range(2):
        project(t, 1)
        project(t, -1)
    for k in range(4):
        for t in range(2):
            l = mod4(m1[t] + lines[k])
            right, left = mod4(m2[t] + 1), mod4(m2[t] - 1)
            to_right, to_left = here.to(axes[t][0], 1), here.to(axes[t][0], -1)
            near_copy[t, k] = [
                copies.start(part_sum.at[1, t, right, l], near_a.at[0, 1, t, k], to_right),
                copies.start(part_sum.at[0, t, left, l], near_a.at[1, 0, t, k], to_left),
            ]
            for copy in far_copy[t, k]:
                copy.wait_recv()
            add(part_sum.at[0, t, right, l], far_a.at[0, t, k])
            add(part_sum.at[1, t, left, l], far_a.at[1, t, k])
            near_copy[t, k] += [
                copies.start(part_sum.at[0, t, right, l], near_a.at[0, 0, t, k], to_right),
                copies.start(part_sum.at[1, t, left, l], near_a.at[1, 1, t, k], to_left),
            ]
        if k == 0:
            for t in range(2):
                project(t, 0)
            for copy in along_z:
                copy.wait_recv()
            behind = route_out.at[here.y, mod4(here.z - 1)]
            far_z = copies.start(behind, behind, here.to("z", 1))

    far_z.wait_recv()
    along_y = ring(route_out.at[here.y], "y")

    def take_near(t, k):
        for copy in near_copy[t, k]:
            copy.wait_recv()
        l = mod4(m1[t] + lines[k])
        for half in range(2):
            add(part_sum.at[half, t, m2[t], l], near_a.at[0, half, t, k], near_a.at[1, half, t, k])

    far_b_copy, near_b_copy = {}, {}
    for t in range(2):
        take_near(t, 0)
        l = mod4(m1[t] + 2)
        far_b_copy[t] = (
            copies.start(part_sum.at[0, t, m2[t], l], far_b.at[0, t], here.to(axes[t][1], 1)),
            copies.start(part_sum.at[1, t, m2[t], l], far_b.at[1, t], here.to(axes[t][1], -1)),
        )
    for k, side, step in ((1, 0, 1), (2, 1, -1)):
        for t in range(2):
            take_near(t, k)
            l = mod4(m1[t] + step)
            far_b_copy[t][side].wait_recv()
            add(part_sum.at[side, t, m2[t], l], far_b.at[side, t])
            near_b_copy[t, side] = copies.start(
                part_sum.at[:, t, m2[t], l], near_b.at[side, :, t], here.to(axes[t][1], step)
            )
    for copy in along_y:
        copy.wait_recv()
    behind = route_out.at[mod4(here.y - 1)]
    far_y = copies.start(behind, behind, here.to("y", 1))
    state_copy.wait_recv()
    square = jnp.zeros((48, 1), F32)
    for t in range(2):
        for copy in near_copy[t, 3]:
            copy.wait_recv()
        for side in range(2):
            near_b_copy[t, side].wait_recv()
        for half in range(2):
            total = part_sum[half, t, m2[t], m1[t]].astype(F32)
            for side in range(2):
                total += near_a[side, half, t, 3].astype(F32)
            for side in range(2):
                total += near_b[side, half, t].astype(F32)
            first = t * 1024 + half * 512
            cols = slice(first, first + 512)
            mine = state_ref[c, :, :, cols]
            theirs = sib_state[:, :, cols]
            low = jnp.where(c == 0, mine, theirs)
            high = jnp.where(c == 0, theirs, mine)
            total += jnp.concatenate([low, high], axis=1).reshape(48, 512)
            res_out[:, :, cols] = total.reshape(SLOTS, 16, 512)
            square += jnp.sum(total * total, axis=1, keepdims=True)
    squares[c] = jnp.broadcast_to(square, (48, 128))
    square_copy = copies.start(squares.at[c], squares.at[c], sib)
    square_copy.wait_recv()
    mean = (squares[0, :, :1] + squares[1, :, :1]) * (1.0 / 4096.0)
    factor = lax.rsqrt(mean + 1e-06).reshape(SLOTS, 16, 1)
    for h in range(2):
        cols = slice(h * 1024, h * 1024 + 1024)
        gain = gain_ref[pl.ds(c, 1), cols].reshape(1, 1, 1024)
        norm_out[h] = (res_out[:, :, cols] * factor * gain).astype(BF)
    far_y.wait_recv()
    copies.finish()


def attention(msg, route, state, gain, out_proj):
    any_space = pl.BlockSpec(memory_space=pl.ANY)
    vmem = pl.BlockSpec(memory_space=pltpu.VMEM)
    count = 15 + 1 + 1 + 1 + 1 + 1 + 2 * (8 + 16 + 2 + 2) + 9 + 1
    return pl.pallas_call(
        attention_kernel,
        out_shape=(
            jax.ShapeDtypeStruct((2, SLOTS, 16, 1024), BF),
            jax.ShapeDtypeStruct((SLOTS, 16, 2048), F32),
            jax.ShapeDtypeStruct((4, 4, 4, 2, 8, 128), F32),
        ),
        in_specs=[vmem, vmem, vmem, vmem, any_space],
        out_specs=(vmem, vmem, vmem),
        scratch_shapes=[
            pltpu.VMEM((2, 16, SLOTS, 2, 16, DH), BF),
            pltpu.VMEM((2, 4, 4, SLOTS, 16, DH), BF),
            pltpu.VMEM((2 * DH, 2048), BF),
            pltpu.VMEM((SLOTS, 8, 2048), F32),
            pltpu.VMEM((2, 2, 4, 4, 48, 512), BF),
            pltpu.VMEM((2, 2, 4, 48, 512), BF),
            pltpu.VMEM((2, 2, 2, 4, 48, 512), BF),
            pltpu.VMEM((2, 2, 48, 512), BF),
            pltpu.VMEM((2, 2, 2, 48, 512), BF),
            pltpu.VMEM((2, 48, 128), F32),
            pltpu.SemaphoreType.DMA((count,)),
            pltpu.SemaphoreType.DMA((count,)),
            pltpu.SemaphoreType.DMA,
        ],
        compiler_params=pltpu.CompilerParams(
            collective_id=3, has_side_effects=True, vmem_limit_bytes=48 * 1024 * 1024
        ),
        name="attention_norm",
    )(msg, route, state, gain, out_proj)


def on_device(
    states, query_in, key_in, value_in, cached_delta, recompute, expert_ids, expert_weights,
    norm_gain, out_proj, gate_proj, up_proj, down_proj,
):
    dev_count = lax.axis_size("dev")
    req_here, seq_here, features = states.shape
    rank = jnp.cumsum(recompute) - 1
    live_count = jnp.sum(recompute)
    idle_rank = live_count + jnp.cumsum(1 - recompute) - 1
    place = jnp.where(recompute == 1, rank, idle_rank)
    pick = (place[None, :] == jnp.arange(SLOTS, dtype=jnp.int32)[:, None]).astype(jnp.int32)
    chosen = jnp.sum(pick * jnp.arange(req_here, dtype=jnp.int32)[None, :], axis=1)
    live_slot = jnp.arange(SLOTS, dtype=jnp.int32) < live_count

    def select(whole):
        return jnp.concatenate(
            [lax.dynamic_slice_in_dim(whole, chosen[s], 1, 0) for s in range(SLOTS)], axis=0
        )

    ids = select(expert_ids.reshape(req_here, seq_here, -1))
    weights = select(expert_weights.reshape(req_here, seq_here, -1))
    experts = jnp.arange(dev_count, dtype=jnp.int32)
    dense = jnp.sum(
        jnp.where(ids[..., None] == experts, weights[..., None], 0.0), axis=2
    )
    dense = jnp.where(live_slot[:, None, None], dense, 0.0)
    route = dense.transpose(1, 0, 2).reshape(seq_here, -1)
    route = jnp.pad(route, ((0, 0), (0, 128 - SLOTS * dev_count)))

    chips = dev_count // 2
    queries = select(query_in).reshape(SLOTS, seq_here, chips, 2, DH).transpose(2, 0, 3, 1, 4)
    keys = select(key_in).reshape(SLOTS, seq_here, KV_HEADS, DH)
    values = select(value_in).reshape(SLOTS, seq_here, KV_HEADS, DH)
    both = jnp.stack([keys, values]).transpose(3, 1, 0, 2, 4)
    both = jnp.repeat(both, chips // KV_HEADS, axis=0)
    msg = jnp.stack(
        [queries.reshape(chips, SLOTS, 16, DH), both.reshape(chips, SLOTS, 16, DH)], axis=2
    )
    state = select(states).astype(F32).reshape(SLOTS, seq_here, 2, 2048).transpose(2, 0, 1, 3)
    normed, residual, routes = attention(msg, route, state, norm_gain.reshape(2, 2048), out_proj)
    fresh = expert_layer(normed, routes, residual, gate_proj[0], up_proj[0], down_proj[0])
    fresh = fresh.transpose(1, 2, 0, 3).reshape(SLOTS, seq_here, features)
    reused = states.astype(jnp.float32) + cached_delta.astype(jnp.float32)
    spread = sum(
        jnp.where((place == s)[:, None, None], fresh[s][None], 0.0) for s in range(SLOTS)
    )
    layer_out = jnp.where((recompute == 1)[:, None, None], spread, reused)
    return layer_out.astype(jnp.bfloat16)


def solution(mesh):
    return jax.shard_map(
        on_device,
        mesh=mesh,
        in_specs=(
            P("grp", "dev", None),
            P("grp", "dev", None),
            P("grp", "dev", None),
            P("grp", "dev", None),
            P("grp", "dev", None),
            P("grp"),
            P(("grp", "dev"), None),
            P(("grp", "dev"), None),
            P(),
            P("dev", None),
            P("dev", None, "grp"),
            P("dev", None, "grp"),
            P("dev", "grp", None),
        ),
        out_specs=P("grp", "dev", None),
        check_vma=False,
    )
```

```python
import math

import jax
import jax.numpy as jnp
from jax import lax
from jax.experimental import pallas as pl
from jax.experimental.pallas import tpu as pltpu
from jax.sharding import PartitionSpec as P

HEADS = 32
KV_HEADS = 8
DH = 128
SLOTS = 3
BF = jnp.bfloat16
F32 = jnp.float32
MESH = pl.DeviceIdType.MESH
ORDER = (("x", "z", "y"), ("z", "y", "x"), ("y", "x", "z"))


def mod4(v):
    return lax.rem(v + 4, 4)


class Place:
    def __init__(self):
        self.y = lax.axis_index("grp")
        dev = lax.axis_index("dev")
        self.core = lax.rem(dev, 2)
        self.x = lax.rem(lax.div(dev, 2), 4)
        self.z = lax.div(dev, 8)

    def at(self, axis):
        return {"x": self.x, "y": self.y, "z": self.z}[axis]

    def to(self, axis, step):
        y, x, z = self.y, self.x, self.z
        if axis == "y":
            y = mod4(y + step)
        elif axis == "x":
            x = mod4(x + step)
        else:
            z = mod4(z + step)
        return (y, (z * 4 + x) * 2 + self.core)

    def sibling(self):
        return (self.y, (self.z * 4 + self.x) * 2 + 1 - self.core)

    def greet(self, axes):
        barrier = pltpu.get_barrier_semaphore()
        others = [self.to(axis, step) for axis in axes for step in (1, -1)]
        others.append(self.sibling())
        for other in others:
            pl.semaphore_signal(barrier, inc=1, device_id=other, device_id_type=MESH)
        pl.semaphore_wait(barrier, len(others))


class Copies:
    def __init__(self, send_sem, recv_sem):
        self.send_sem, self.recv_sem = send_sem, recv_sem
        self.made, self.count = [], 0

    def start(self, src, dst, device):
        k = self.count
        self.count += 1
        copy = pltpu.make_async_remote_copy(
            src_ref=src,
            dst_ref=dst,
            send_sem=self.send_sem.at[k],
            recv_sem=self.recv_sem.at[k],
            device_id=device,
            device_id_type=MESH,
        )
        copy.start()
        self.made.append(copy)
        return copy

    def finish(self):
        for copy in self.made:
            copy.wait_send()


def experts_kernel(
    norm_ref, route_ref, res_ref, gate_hbm, up_hbm, down_hbm,
    out_ref,
    tok, wg, wu, hv, dw, free3, fin, send_sem, recv_sem, load_sem, ready,
):
    here = Place()
    c = here.core
    sib = here.sibling()
    my_half = pl.ds(pl.multiple_of(c * 2048, 2048), 2048)
    load_g = pltpu.make_async_copy(gate_hbm, wg, load_sem.at[0])
    load_u = pltpu.make_async_copy(up_hbm, wu, load_sem.at[1])
    load_d = pltpu.make_async_copy(down_hbm.at[:, my_half], dw.at[c], load_sem.at[2])
    load_g.start()
    load_u.start()
    load_d.start()
    here.greet(("x", "y", "z"))
    copies = Copies(send_sem, recv_sem)
    m1 = [here.at(ORDER[p][0]) for p in range(SLOTS)]
    m2 = [here.at(ORDER[p][1]) for p in range(SLOTS)]
    m3 = [here.at(ORDER[p][2]) for p in range(SLOTS)]
    parts = range(SLOTS)

    def to(p, axis_at, step):
        return here.to(ORDER[p][axis_at - 1], step)

    other_half = pl.ds(pl.multiple_of((1 - c) * 2048, 2048), 2048)
    pair = pl.ds(2 * c, 2)
    for p in parts:
        for h in range(2):
            tok[2 * c + h, p, m3[p], m2[p], m1[p]] = norm_ref[h, p]

    moved = []

    def send(region, device):
        moved.append(copies.start(region, region, device))
        return moved[-1]

    first = []
    for p in parts:
        block = tok.at[pair, p, m3[p], m2[p], m1[p]]
        first.append((send(block, to(p, 1, 1)), send(block, to(p, 1, -1))))
    second = []
    for p in parts:
        for copy in first[p]:
            copy.wait_recv()
        second.append((
            send(tok.at[2 * c, p, m3[p], m2[p], mod4(m1[p] - 1)], to(p, 1, 1)),
            send(tok.at[2 * c + 1, p, m3[p], m2[p], mod4(m1[p] + 1)], to(p, 1, -1)),
        ))

    def line(p, c3, c2):
        return tok.at[pair, p, c3, c2]

    own_line = [{} for p in parts]
    ring2 = []
    subs = [[None] * 4 for p in parts]
    offsets = (0, 1, -1, 2)
    for p in parts:
        for copy in second[p]:
            copy.wait_recv()
        region = line(p, m3[p], m2[p])
        ring2.append((send(region, to(p, 2, 1)), send(region, to(p, 2, -1))))
        own_line[p][0] = send(region, sib)
    for p in parts:
        region = line(p, m3[p], m2[p])
        subs[p][0] = (send(region, to(p, 3, 1)), send(region, to(p, 3, -1)))
    ring2b = []
    for p in parts:
        for copy in ring2[p]:
            copy.wait_recv()
        ring2b.append((
            send(tok.at[2 * c, p, m3[p], mod4(m2[p] - 1)], to(p, 2, 1)),
            send(tok.at[2 * c + 1, p, m3[p], mod4(m2[p] + 1)], to(p, 2, -1)),
        ))
        for j in (1, 2):
            own_line[p][j] = send(line(p, m3[p], mod4(m2[p] + offsets[j])), sib)
    for j in (1, 2):
        for p in parts:
            region = line(p, m3[p], mod4(m2[p] + offsets[j]))
            subs[p][j] = (send(region, to(p, 3, 1)), send(region, to(p, 3, -1)))

    load_g.wait()
    load_u.wait()

    handed = [[] for p in parts]
    expert = lax.axis_index("dev")
    lane = lax.broadcasted_iota(jnp.int32, (64, 128), 1)

    def weight_of(p, c3, c2):
        index = ((c3, c2), (c2, slice(None), c3), (slice(None), c3, c2))[p]
        held = route_ref[index].reshape(64, 128)
        return jnp.sum(jnp.where(lane == p * 32 + expert, held, 0.0), axis=1, keepdims=True)

    def ffn(pieces):
        weights = [weight_of(*piece) for piece in pieces]

        def tile(n, carry):
            cols = pl.ds(pl.multiple_of(n * 256, 256), 256)
            gate = jnp.zeros((64 * len(pieces), 256), F32)
            up = jnp.zeros((64 * len(pieces), 256), F32)
            for q in range(4):
                rows = jnp.concatenate([tok[q, p, c3, c2].reshape(64, 1024) for p, c3, c2 in pieces], axis=0)
                depth = pl.ds(q * 1024, 1024)
                gate += jnp.dot(rows, wg[depth, cols], preferred_element_type=F32)
                up += jnp.dot(rows, wu[depth, cols], preferred_element_type=F32)
            act = gate / (1.0 + jnp.exp(-gate)) * up
            for i, (p, c3, c2) in enumerate(pieces):
                hv[c, p, c3, c2, :, cols] = (act[64 * i : 64 * i + 64] * weights[i]).astype(BF)
            return carry

        lax.fori_loop(0, 3, tile, 0)
        for p, c3, c2 in pieces:
            piece = hv.at[c, p, c3, c2]
            handed[p].append(copies.start(piece, piece, sib))

    def own_unit(lines):
        for p in parts:
            for j in lines:
                own_line[p][j].wait_recv()
        ffn([(p, m3[p], mod4(m2[p] + offsets[j])) for p in parts for j in lines])

    passed = [[None] * 4 for p in parts]
    onward = [[None] * 4 for p in parts]
    opposite = [[None] * 4 for p in parts]

    def forward(j):
        for p in parts:
            line_at = mod4(m2[p] + offsets[j])
            left, right = mod4(m3[p] - 1), mod4(m3[p] + 1)
            for copy in subs[p][j]:
                copy.wait_recv()
            onward[p][j] = (
                send(tok.at[2 * c, p, left, line_at], to(p, 3, 1)),
                send(tok.at[2 * c + 1, p, right, line_at], to(p, 3, -1)),
            )
            passed[p][j] = (send(line(p, left, line_at), sib), send(line(p, right, line_at), sib))

    def near_unit(j):
        for p in parts:
            for copy in passed[p][j]:
                copy.wait_recv()
        ffn([(p, mod4(m3[p] + side), mod4(m2[p] + offsets[j])) for p in parts for side in (-1, 1)])

    def settle(j):
        for p in parts:
            for copy in onward[p][j]:
                copy.wait_recv()
            opposite[p][j] = send(line(p, mod4(m3[p] + 2), mod4(m2[p] + offsets[j])), sib)

    def far_unit(lines):
        for p in parts:
            for j in lines:
                opposite[p][j].wait_recv()
        ffn([(p, mod4(m3[p] + 2), mod4(m2[p] + offsets[j])) for p in parts for j in lines])

    def part(n, p, c3, c2):
        return tok.at[2 * (1 - c) + n, p, c3, c2]

    both = pl.ds(2 * (1 - c), 2)

    def down(p, off, n):
        at = mod4(m3[p] + off)
        total = jnp.dot(hv[0, p, at].reshape(256, 768), dw[0, :, n * 1024 : n * 1024 + 1024], preferred_element_type=F32)
        total += jnp.dot(hv[1, p, at].reshape(256, 768), dw[1, :, n * 1024 : n * 1024 + 1024], preferred_element_type=F32)
        tok[2 * (1 - c) + n, p, at] = total.astype(BF).reshape(4, 4, 16, 1024)

    def add(ref, *others):
        total = ref[...].astype(F32)
        for other in others:
            total += other[...].astype(F32)
        ref[...] = total.astype(BF)

    lines = (2, 1, -1, 0)

    def at_line(p, k):
        return mod4(m2[p] + lines[k])

    def take_handed():
        for p in parts:
            for copy in handed[p]:
                copy.wait_recv()
            handed[p].clear()

    far_copy, near_copy = {}, {}

    def pass_free(p, k):
        l = at_line(p, k)
        right, left = mod4(m3[p] + 1), mod4(m3[p] - 1)
        near_copy[p, k] = [
            copies.start(part(1, p, right, l), free3.at[0, p, k], to(p, 3, 1)),
            copies.start(part(0, p, left, l), free3.at[1, p, k], to(p, 3, -1)),
        ]

    def pass_far(p, k):
        at, l = mod4(m3[p] + 2), at_line(p, k)
        far_copy[p, k] = (
            copies.start(part(0, p, at, l), tok.at[2 * c, p, 0, k], to(p, 3, 1)),
            copies.start(part(1, p, at, l), tok.at[2 * c + 1, p, 0, k], to(p, 3, -1)),
        )

    def pass_bound(p, k):
        l = at_line(p, k)
        right, left = mod4(m3[p] + 1), mod4(m3[p] - 1)
        for copy in far_copy[p, k]:
            copy.wait_recv()
        add(part(0, p, right, l), tok.at[2 * c, p, 0, k])
        add(part(1, p, left, l), tok.at[2 * c + 1, p, 0, k])
        near_copy[p, k] += [
            copies.start(part(0, p, right, l), tok.at[2 * c, p, 1, k], to(p, 3, 1)),
            copies.start(part(1, p, left, l), tok.at[2 * c + 1, p, 1, k], to(p, 3, -1)),
        ]

    def take_near(p, k):
        for copy in near_copy[p, k]:
            copy.wait_recv()
        l = at_line(p, k)
        add(part(0, p, m3[p], l), tok.at[2 * c, p, 1, k], free3.at[1, p, k])
        add(part(1, p, m3[p], l), tok.at[2 * c + 1, p, 1, k], free3.at[0, p, k])

    own_unit((0, 1))
    for p in parts:
        for copy in ring2b[p]:
            copy.wait_recv()
        region = line(p, m3[p], mod4(m2[p] + 2))
        subs[p][3] = (send(region, to(p, 3, 1)), send(region, to(p, 3, -1)))
        own_line[p][3] = send(region, sib)
    forward(0)
    own_unit((2, 3))
    down_copy = copies.start(down_hbm.at[:, other_half], dw.at[c], sib)
    forward(1)
    near_unit(0)
    forward(2)
    near_unit(1)
    forward(3)
    near_unit(2)
    settle(0)
    settle(1)
    near_unit(3)
    settle(2)
    settle(3)
    load_d.wait()
    down_copy.wait_recv()
    take_handed()
    for p in parts:
        down(p, 1, 1)
        down(p, -1, 0)
        for k in range(4):
            pass_free(p, k)
    far_unit((0, 1))
    far_unit((2, 3))
    for copy in moved:
        copy.wait_send()
    done = [id(copy) for copy in moved]
    copies.made = [copy for copy in copies.made if id(copy) not in done]
    neighbours = [here.to(axis, step) for axis in ("x", "y", "z") for step in (1, -1)]
    for other in neighbours:
        pl.semaphore_signal(ready, inc=1, device_id=other, device_id_type=MESH)
    take_handed()
    for p in parts:
        down(p, 2, 0)
        down(p, 2, 1)
        if p == 0:
            pl.semaphore_wait(ready, len(neighbours))
        for k in range(4):
            pass_far(p, k)
    for p in parts:
        down(p, 1, 0)
        down(p, -1, 1)
    for k in range(2):
        for p in parts:
            pass_bound(p, k)
    for p in parts:
        down(p, 0, 0)
        down(p, 0, 1)
    far2_copy, near2_copy = {}, {}
    for p in parts:
        take_near(p, 0)
        l = at_line(p, 0)
        far2_copy[p] = (
            copies.start(part(0, p, m3[p], l), tok.at[2 * c, p, 2, 0], to(p, 2, 1)),
            copies.start(part(1, p, m3[p], l), tok.at[2 * c + 1, p, 2, 0], to(p, 2, -1)),
        )
    for k in (2, 3):
        for p in parts:
            pass_bound(p, k)
    for k, side in ((1, 0), (2, 1)):
        for p in parts:
            take_near(p, k)
            l = at_line(p, k)
            far2_copy[p][side].wait_recv()
            add(part(side, p, m3[p], l), tok.at[2 * c + side, p, 2, 0])
            near2_copy[p, side] = copies.start(
                tok.at[both, p, m3[p], l], tok.at[2 * c + side, p, 2, pl.ds(1, 2)], to(p, 2, 1 if side == 0 else -1)
            )
    far1_copy, near1_copy = {}, {}
    for p in parts:
        take_near(p, 3)
    for p in parts:
        for side in range(2):
            near2_copy[p, side].wait_recv()
        for q in range(2):
            add(part(q, p, m3[p], m2[p]), tok.at[2 * c, p, 2, 1 + q], tok.at[2 * c + 1, p, 2, 1 + q])
        far = mod4(m1[p] + 2)
        far1_copy[p] = (
            copies.start(part(0, p, m3[p], m2[p]).at[far], tok.at[2 * c, p, 3, 0, 0], to(p, 1, 1)),
            copies.start(part(1, p, m3[p], m2[p]).at[far], tok.at[2 * c + 1, p, 3, 0, 0], to(p, 1, -1)),
        )
    for p in parts:
        for side, step in ((0, 1), (1, -1)):
            near = mod4(m1[p] + step)
            far1_copy[p][side].wait_recv()
            add(part(side, p, m3[p], m2[p]).at[near], tok.at[2 * c + side, p, 3, 0, 0])
            near1_copy[p, side] = copies.start(
                tok.at[both, p, m3[p], m2[p], near], tok.at[2 * c + side, p, 3, 1, pl.ds(0, 2)], to(p, 1, step)
            )
    for p in parts:
        for side in range(2):
            near1_copy[p, side].wait_recv()
        for q in range(2):
            total = tok[2 * (1 - c) + q, p, m3[p], m2[p], m1[p]].astype(F32)
            for side in range(2):
                total += tok[2 * c + side, p, 3, 1, q].astype(F32)
            total += res_ref[p, :, q * 1024 : q * 1024 + 1024]
            fin[0, p, :, q * 1024 : q * 1024 + 1024] = total[:8]
            fin[1, p, :, q * 1024 : q * 1024 + 1024] = total[8:]
    last = copies.start(fin.at[1 - c], out_ref.at[c], sib)
    out_ref[c] = fin[c]
    last.wait_recv()
    copies.finish()


def expert_layer(normed, route, residual, gate_w, up_w, down_w):
    any_space = pl.BlockSpec(memory_space=pl.ANY)
    vmem = pl.BlockSpec(memory_space=pltpu.VMEM)
    count = SLOTS * (4 + 4 + 16 + 16 + 16) + 1 + SLOTS * (8 + 16 + 4 + 4) + 1
    return pl.pallas_call(
        experts_kernel,
        out_shape=jax.ShapeDtypeStruct((2, SLOTS, 8, 2048), F32),
        in_specs=[vmem, vmem, vmem, any_space, any_space, any_space],
        out_specs=vmem,
        scratch_shapes=[
            pltpu.VMEM((4, SLOTS, 4, 4, 4, 16, 1024), BF),
            pltpu.VMEM((4096, 768), BF),
            pltpu.VMEM((4096, 768), BF),
            pltpu.VMEM((2, SLOTS, 4, 4, 64, 768), BF),
            pltpu.VMEM((2, 768, 2048), BF),
            pltpu.VMEM((2, SLOTS, 4, 4, 16, 1024), BF),
            pltpu.VMEM((2, SLOTS, 8, 2048), F32),
            pltpu.SemaphoreType.DMA((count,)),
            pltpu.SemaphoreType.DMA((count,)),
            pltpu.SemaphoreType.DMA((3,)),
            pltpu.SemaphoreType.REGULAR,
        ],
        compiler_params=pltpu.CompilerParams(
            collective_id=1, has_side_effects=True, vmem_limit_bytes=60 * 1024 * 1024
        ),
        name="experts_kernel",
    )(normed, route, residual, gate_w, up_w, down_w)


def attend(q, k, v):
    scores = lax.dot_general(q, k, (((1,), (1,)), ((), ())), preferred_element_type=F32)
    scores = scores * (1.0 / math.sqrt(DH))
    raised = jnp.exp(scores - jnp.max(scores, axis=-1, keepdims=True))
    weights = (raised / jnp.sum(raised, axis=-1, keepdims=True)).astype(BF)
    return jnp.dot(weights, v, preferred_element_type=F32)


def attention_kernel(
    msg, route_ref, state_ref, gain_ref, proj_hbm,
    norm_out, res_out, route_out,
    got, mixed, ow, sib_state, part_sum, far_a, near_a, far_b, near_b, squares,
    send_sem, recv_sem, load_sem,
):
    here = Place()
    c = here.core
    sib = here.sibling()
    chip = here.z * 4 + here.x

    my_half = pl.ds(pl.multiple_of(c * 2048, 2048), 2048)
    other_half = pl.ds(pl.multiple_of((1 - c) * 2048, 2048), 2048)
    my_rows = pl.ds(pl.multiple_of(c * DH, DH), DH)
    load = pltpu.make_async_copy(proj_hbm.at[:, my_half], ow.at[my_rows], load_sem)
    load.start()

    hops = [(dz, dx) for dz in range(4) for dx in range(4) if (dz, dx) != (0, 0)]
    hops.sort(key=lambda hop: -(min(hop[0], 4 - hop[0]) + min(hop[1], 4 - hop[1])))

    def chip_at(dz, dx):
        return lax.rem(here.z + dz, 4) * 4 + lax.rem(here.x + dx, 4)

    barrier = pltpu.get_barrier_semaphore()
    others = [(here.y, chip_at(dz, dx) * 2 + c) for dz, dx in hops]
    greeted = others + [here.to("y", 1), here.to("y", -1), sib]
    for other in greeted:
        pl.semaphore_signal(barrier, inc=1, device_id=other, device_id_type=MESH)
    pl.semaphore_wait(barrier, len(greeted))

    copies = Copies(send_sem, recv_sem)
    arriving = []
    for (dz, dx), other in zip(hops, others):
        arriving.append(copies.start(msg.at[chip_at(dz, dx)], got.at[c, chip], other))
    got[c, chip] = msg[chip]
    route_out[here.y, here.z, here.x, c] = route_ref[...]
    tile = route_out.at[here.y, here.z, here.x, c]
    route_swap = copies.start(tile, tile, sib)
    proj_copy = copies.start(proj_hbm.at[:, other_half], ow.at[my_rows], sib)
    state_copy = copies.start(state_ref.at[1 - c], sib_state, sib)

    def ring(region, axis):
        return (copies.start(region, region, here.to(axis, 1)), copies.start(region, region, here.to(axis, -1)))

    route_swap.wait_recv()
    along_x = ring(route_out.at[here.y, here.z, here.x], "x")
    for copy in arriving:
        copy.wait_recv()
    passed = copies.start(got.at[c], got.at[c], sib)
    for copy in along_x:
        copy.wait_recv()
    left = route_out.at[here.y, here.z, mod4(here.x - 1)]
    far_x = copies.start(left, left, here.to("x", 1))
    passed.wait_recv()
    for s in range(SLOTS):
        held = got[:, :, s].astype(F32)
        q = jnp.where(c == 0, held[:, :, 0, :8], held[:, :, 0, 8:]).reshape(256, DH).astype(BF)
        k = held[:, :, 1, :8].reshape(256, DH).astype(BF)
        v = held[:, :, 1, 8:].reshape(256, DH).astype(BF)
        out = attend(q, k, v).reshape(2, 4, 4, 8, DH)
        mixed[c, :, :, s] = jnp.concatenate([out[0], out[1]], axis=2).astype(BF)
    mixed_copy = copies.start(mixed.at[c], mixed.at[c], sib)
    far_x.wait_recv()
    along_z = ring(route_out.at[here.y, here.z], "z")
    load.wait()
    proj_copy.wait_recv()
    mixed_copy.wait_recv()

    axes = (("z", "x"), ("x", "z"))
    m2 = [here.at(axes[t][0]) for t in range(2)]
    m1 = [here.at(axes[t][1]) for t in range(2)]

    def project(t, off):
        at = mod4(m2[t] + off)
        rows = [(mixed[h, at] if t == 0 else mixed[h, :, at]).reshape(192, DH) for h in range(2)]
        rows = jnp.concatenate(rows, axis=1)
        for half in range(2):
            first = t * 1024 + half * 512
            total = jnp.dot(rows, ow[:, first : first + 512], preferred_element_type=F32)
            part_sum[half, t, at] = total.astype(BF).reshape(4, 48, 512)

    def add(ref, *terms):
        total = ref[...].astype(F32)
        for term in terms:
            total += term[...].astype(F32)
        ref[...] = total.astype(BF)

    lines = (2, 1, -1, 0)
    far_copy, near_copy = {}, {}
    for t in range(2):
        project(t, 2)
        at = mod4(m2[t] + 2)
        for k in range(4):
            l = mod4(m1[t] + lines[k])
            far_copy[t, k] = (
                copies.start(part_sum.at[0, t, at, l], far_a.at[0, t, k], here.to(axes[t][0], 1)),
                copies.start(part_sum.at[1, t, at, l], far_a.at[1, t, k], here.to(axes[t][0], -1)),
            )
    for t in range(2):
        project(t, 1)
        project(t, -1)
    for k in range(4):
        for t in range(2):
            l = mod4(m1[t] + lines[k])
            right, left = mod4(m2[t] + 1), mod4(m2[t] - 1)
            to_right, to_left = here.to(axes[t][0], 1), here.to(axes[t][0], -1)
            near_copy[t, k] = [
                copies.start(part_sum.at[1, t, right, l], near_a.at[0, 1, t, k], to_right),
                copies.start(part_sum.at[0, t, left, l], near_a.at[1, 0, t, k], to_left),
            ]
            for copy in far_copy[t, k]:
                copy.wait_recv()
            add(part_sum.at[0, t, right, l], far_a.at[0, t, k])
            add(part_sum.at[1, t, left, l], far_a.at[1, t, k])
            near_copy[t, k] += [
                copies.start(part_sum.at[0, t, right, l], near_a.at[0, 0, t, k], to_right),
                copies.start(part_sum.at[1, t, left, l], near_a.at[1, 1, t, k], to_left),
            ]
        if k == 0:
            for t in range(2):
                project(t, 0)
            for copy in along_z:
                copy.wait_recv()
            behind = route_out.at[here.y, mod4(here.z - 1)]
            far_z = copies.start(behind, behind, here.to("z", 1))

    far_z.wait_recv()
    along_y = ring(route_out.at[here.y], "y")

    def take_near(t, k):
        for copy in near_copy[t, k]:
            copy.wait_recv()
        l = mod4(m1[t] + lines[k])
        for half in range(2):
            add(part_sum.at[half, t, m2[t], l], near_a.at[0, half, t, k], near_a.at[1, half, t, k])

    far_b_copy, near_b_copy = {}, {}
    for t in range(2):
        take_near(t, 0)
        l = mod4(m1[t] + 2)
        far_b_copy[t] = (
            copies.start(part_sum.at[0, t, m2[t], l], far_b.at[0, t], here.to(axes[t][1], 1)),
            copies.start(part_sum.at[1, t, m2[t], l], far_b.at[1, t], here.to(axes[t][1], -1)),
        )
    for k, side, step in ((1, 0, 1), (2, 1, -1)):
        for t in range(2):
            take_near(t, k)
            l = mod4(m1[t] + step)
            far_b_copy[t][side].wait_recv()
            add(part_sum.at[side, t, m2[t], l], far_b.at[side, t])
            near_b_copy[t, side] = copies.start(
                part_sum.at[:, t, m2[t], l], near_b.at[side, :, t], here.to(axes[t][1], step)
            )
    for copy in along_y:
        copy.wait_recv()
    behind = route_out.at[mod4(here.y - 1)]
    far_y = copies.start(behind, behind, here.to("y", 1))
    state_copy.wait_recv()
    square = jnp.zeros((48, 1), F32)
    for t in range(2):
        for copy in near_copy[t, 3]:
            copy.wait_recv()
        for side in range(2):
            near_b_copy[t, side].wait_recv()
        for half in range(2):
            total = part_sum[half, t, m2[t], m1[t]].astype(F32)
            for side in range(2):
                total += near_a[side, half, t, 3].astype(F32)
            for side in range(2):
                total += near_b[side, half, t].astype(F32)
            first = t * 1024 + half * 512
            cols = slice(first, first + 512)
            mine = state_ref[c, :, :, cols]
            theirs = sib_state[:, :, cols]
            low = jnp.where(c == 0, mine, theirs)
            high = jnp.where(c == 0, theirs, mine)
            total += jnp.concatenate([low, high], axis=1).reshape(48, 512)
            res_out[:, :, cols] = total.reshape(SLOTS, 16, 512)
            square += jnp.sum(total * total, axis=1, keepdims=True)
    squares[c] = jnp.broadcast_to(square, (48, 128))
    square_copy = copies.start(squares.at[c], squares.at[c], sib)
    square_copy.wait_recv()
    mean = (squares[0, :, :1] + squares[1, :, :1]) * (1.0 / 4096.0)
    factor = lax.rsqrt(mean + 1e-06).reshape(SLOTS, 16, 1)
    for h in range(2):
        cols = slice(h * 1024, h * 1024 + 1024)
        gain = gain_ref[pl.ds(c, 1), cols].reshape(1, 1, 1024)
        norm_out[h] = (res_out[:, :, cols] * factor * gain).astype(BF)
    far_y.wait_recv()
    copies.finish()


def attention(msg, route, state, gain, out_proj):
    any_space = pl.BlockSpec(memory_space=pl.ANY)
    vmem = pl.BlockSpec(memory_space=pltpu.VMEM)
    count = 15 + 1 + 1 + 1 + 1 + 1 + 2 * (8 + 16 + 2 + 2) + 9 + 1
    return pl.pallas_call(
        attention_kernel,
        out_shape=(
            jax.ShapeDtypeStruct((2, SLOTS, 16, 1024), BF),
            jax.ShapeDtypeStruct((SLOTS, 16, 2048), F32),
            jax.ShapeDtypeStruct((4, 4, 4, 2, 8, 128), F32),
        ),
        in_specs=[vmem, vmem, vmem, vmem, any_space],
        out_specs=(vmem, vmem, vmem),
        scratch_shapes=[
            pltpu.VMEM((2, 16, SLOTS, 2, 16, DH), BF),
            pltpu.VMEM((2, 4, 4, SLOTS, 16, DH), BF),
            pltpu.VMEM((2 * DH, 2048), BF),
            pltpu.VMEM((SLOTS, 8, 2048), F32),
            pltpu.VMEM((2, 2, 4, 4, 48, 512), BF),
            pltpu.VMEM((2, 2, 4, 48, 512), BF),
            pltpu.VMEM((2, 2, 2, 4, 48, 512), BF),
            pltpu.VMEM((2, 2, 48, 512), BF),
            pltpu.VMEM((2, 2, 2, 48, 512), BF),
            pltpu.VMEM((2, 48, 128), F32),
            pltpu.SemaphoreType.DMA((count,)),
            pltpu.SemaphoreType.DMA((count,)),
            pltpu.SemaphoreType.DMA,
        ],
        compiler_params=pltpu.CompilerParams(
            collective_id=3, has_side_effects=True, vmem_limit_bytes=48 * 1024 * 1024
        ),
        name="attention_norm",
    )(msg, route, state, gain, out_proj)


def on_device(
    states, query_in, key_in, value_in, cached_delta, recompute, expert_ids, expert_weights,
    norm_gain, out_proj, gate_proj, up_proj, down_proj,
):
    dev_count = lax.axis_size("dev")
    req_here, seq_here, features = states.shape
    counted = jnp.arange(req_here)[:, None] >= jnp.arange(req_here)[None, :]
    rank = jnp.sum(jnp.where(counted, recompute[None, :], 0), axis=1) - 1
    live_count = jnp.sum(recompute)
    idle_rank = live_count + jnp.sum(jnp.where(counted, 1 - recompute[None, :], 0), axis=1) - 1
    place = jnp.where(recompute == 1, rank, idle_rank)
    live_slot = jnp.arange(SLOTS, dtype=jnp.int32) < live_count

    match = place[None, :] == jnp.arange(SLOTS, dtype=jnp.int32)[:, None]

    def select(whole):
        value = jnp.broadcast_to(whole[:1], (SLOTS,) + whole.shape[1:])
        for i in range(1, req_here):
            value = jnp.where(match[:, i].reshape(SLOTS, 1, 1), whole[i : i + 1], value)
        return value

    ids = select(expert_ids.reshape(req_here, seq_here, -1))
    weights = select(expert_weights.reshape(req_here, seq_here, -1))
    experts = jnp.arange(dev_count, dtype=jnp.int32)
    dense = jnp.sum(
        jnp.where(ids[..., None] == experts, weights[..., None], 0.0), axis=2
    )
    dense = jnp.where(live_slot[:, None, None], dense, 0.0)
    route = dense.transpose(1, 0, 2).reshape(seq_here, -1)
    route = jnp.pad(route, ((0, 0), (0, 128 - SLOTS * dev_count)))

    chips = dev_count // 2
    queries = select(query_in).reshape(SLOTS, seq_here, chips, 2, DH).transpose(2, 0, 3, 1, 4)
    keys = select(key_in).reshape(SLOTS, seq_here, KV_HEADS, DH)
    values = select(value_in).reshape(SLOTS, seq_here, KV_HEADS, DH)
    both = jnp.stack([keys, values]).transpose(3, 1, 0, 2, 4)
    both = jnp.repeat(both, chips // KV_HEADS, axis=0)
    msg = jnp.stack(
        [queries.reshape(chips, SLOTS, 16, DH), both.reshape(chips, SLOTS, 16, DH)], axis=2
    )
    state = select(states).astype(F32).reshape(SLOTS, seq_here, 2, 2048).transpose(2, 0, 1, 3)
    normed, residual, routes = attention(msg, route, state, norm_gain.reshape(2, 2048), out_proj)
    fresh = expert_layer(normed, routes, residual, gate_proj[0], up_proj[0], down_proj[0])
    fresh = fresh.transpose(1, 2, 0, 3).reshape(SLOTS, seq_here, features)
    reused = states.astype(jnp.float32) + cached_delta.astype(jnp.float32)
    spread = sum(
        jnp.where((place == s)[:, None, None], fresh[s][None], 0.0) for s in range(SLOTS)
    )
    layer_out = jnp.where((recompute == 1)[:, None, None], spread, reused)
    return layer_out.astype(jnp.bfloat16)


def solution(mesh):
    return jax.shard_map(
        on_device,
        mesh=mesh,
        in_specs=(
            P("grp", "dev", None),
            P("grp", "dev", None),
            P("grp", "dev", None),
            P("grp", "dev", None),
            P("grp", "dev", None),
            P("grp"),
            P(("grp", "dev"), None),
            P(("grp", "dev"), None),
            P(),
            P("dev", None),
            P("dev", None, "grp"),
            P("dev", None, "grp"),
            P("dev", "grp", None),
        ),
        out_specs=P("grp", "dev", None),
        check_vma=False,
    )
```
